256 devices in a mesh: dp: 16 (over y, z_hi, core), fsdp: 16 (over z_lo, x).
Axes of the slice: x: 4, y: 4, z: 8 (z_hi: 2, z_lo: 4; z = z_hi * 4 + z_lo), core: 2. Of those that a mesh axis runs over, the one named last changes fastest.
Arguments:
- tokens: bfloat16 [8192, 5120], P('dp', 'fsdp'), may hold values from -6 to 6
- norm_gain: float32 [5120], replicated, may hold values from 0.25 to 1.75
- expansion: bfloat16 [5120, 4096], P(None, 'fsdp'), may hold values from -0.078125 to 0.078125
- small_weight: bfloat16 [4096, 4096], P(None, 'fsdp'), may hold values from -0.09375 to 0.09375
- cotangent: bfloat16 [8192, 5120], P('dp', 'fsdp'), may hold values from -6 to 6
Outputs:
- mixed: bfloat16 [8192, 5120], P('dp', 'fsdp')
- operator_grad: float32 [5120, 4096], P(None, 'fsdp')
The draws below stay inside these ranges and needn't reach their ends.
All inputs are finite; a program needn't handle non-finite values.
Results may differ from the reference program's by a relative error of at most 0.0058.
Values may be sent and summed in bfloat16 or wider, within the bound.
A program may use at most 128 MiB of HBM per device.

```python
import jax
import jax.numpy as jnp
from jax import lax

D = 5120
DS = 4096
TOKENS = 8192


def block_levels(key, extent, pieces, smallest, largest):
    loudness = 1.0
    for axis_at, blocks in pieces:
        draws = jax.random.uniform(jax.random.fold_in(jax.random.fold_in(key, 6), axis_at), (blocks,), jnp.float32, smallest / len(pieces), largest / len(pieces))
        loudness = loudness * jnp.repeat(jnp.exp(draws), extent[axis_at] // blocks).reshape((-1,) + (1,) * (len(extent) - 1 - axis_at))
    return loudness


def centred(stream_key, shape, scale, bound, split=(), dtype=jnp.bfloat16):
    gain = block_levels(stream_key, shape, split, -0.22, 0.18) if split else 1.0
    drawn = jax.random.normal(stream_key, shape, jnp.float32) * scale * gain
    return jnp.minimum(jnp.maximum(drawn, -bound), bound).astype(dtype)


def setup_inputs(seed: int = 0) -> dict:
    keys = jax.random.split(jax.random.key(seed), 6)
    tokens = centred(keys[0], (TOKENS, D), 1.0, 6.0, ((0, 16), (1, 16)))
    norm_gain = jnp.clip(1.0 + 0.15 * jax.random.normal(keys[1], (D,), jnp.float32), 0.25, 1.75)
    expansion = centred(keys[2], (D, DS), D ** -0.5, 0.078125, ((1, 16),))
    small_weight = centred(keys[3], (DS, DS), DS ** -0.5, 0.09375, ((1, 16),))
    cotangent = centred(keys[4], (TOKENS, D), 1.0, 6.0, ((0, 16), (1, 16)))
    return {"tokens": tokens, "norm_gain": norm_gain, "expansion": expansion, "small_weight": small_weight, "cotangent": cotangent}


def reference(tokens, norm_gain, expansion, small_weight, cotangent):
    wide = tokens.astype(jnp.float32)
    scale = lax.rsqrt(lax.optimization_barrier(jnp.mean(wide * wide, axis=1, keepdims=True)) + 1e-05)
    normed = (wide * scale * norm_gain[None, :]).astype(jnp.bfloat16)
    reduced = jnp.dot(normed, expansion, preferred_element_type=jnp.float32).astype(jnp.bfloat16)
    projected = jnp.dot(reduced, small_weight.T, preferred_element_type=jnp.float32).astype(jnp.bfloat16)
    mixed = (wide + jnp.dot(projected, expansion.T, preferred_element_type=jnp.float32)).astype(jnp.bfloat16)
    back_small = jnp.dot(cotangent, expansion, preferred_element_type=jnp.float32).astype(jnp.bfloat16)
    back_reduced = jnp.dot(back_small, small_weight, preferred_element_type=jnp.float32).astype(jnp.bfloat16)
    grad = jnp.dot(cotangent.T, projected, preferred_element_type=jnp.float32)
    grad = grad + jnp.dot(normed.T, back_reduced, preferred_element_type=jnp.float32)
    return (mixed, grad)
```

```python
import jax
import jax.numpy as jnp
from jax import lax
from jax.experimental import pallas as pl
from jax.experimental.pallas import tpu as pltpu
from jax.sharding import PartitionSpec as P

MESH = pl.DeviceIdType.MESH
F32 = jnp.float32
BF16 = jnp.bfloat16
N_SEMS = 160


def nn(a, b):
    return lax.dot_general(a, b, (((1,), (0,)), ((), ())), preferred_element_type=F32)


def nt(a, b):
    return lax.dot_general(a, b, (((1,), (1,)), ((), ())), preferred_element_type=F32)


def kernel(
    x_ref, gain_ref, e_ref, w_ref, c_ref, mixed_ref, fg,
    stat_x, stat_z, gx, gc, normed, eb, ebt, wb, wbt,
    r_s, r_r, r_g, p_s, p_r, p_g, b_s, b_r, b_g, q_s, q_r, q_g,
    o_s, o_r, acc, o_own, grad, gs, gr, ys, yr, zs, zr, y_own, z_own, x_s,
    ss, rs, ls,
):
    chunk, tok = x_ref.shape
    sub = w_ref.shape[2]
    features = chunk * 16
    d, f = lax.axis_index("dp"), lax.axis_index("fsdp")
    y, h, c = d // 4, (d // 2) % 2, d % 2
    z, x = f // 4, f % 4

    def dev(y=y, h=h, c=c, z=z, x=x):
        return {"dp": y * 4 + h * 2 + c, "fsdp": z * 4 + x}

    def turn(v, k):
        return lax.rem(v + k + 4, 4)

    xp = [dev(x=turn(x, k)) for k in range(4)]
    zp = [dev(z=turn(z, k)) for k in range(4)]
    yp = [dev(y=turn(y, k)) for k in range(4)]
    hp, cp = dev(h=1 - h), dev(c=1 - c)
    right, left = dev(z=jnp.minimum(z + 1, 3)), dev(z=jnp.maximum(z - 1, 0))

    barrier = pltpu.get_barrier_semaphore()
    friends = xp[1:] + zp[1:] + yp[1:] + [hp, cp]
    for friend in friends:
        pl.semaphore_signal(barrier, inc=1, device_id=friend, device_id_type=MESH)
    pl.semaphore_wait(barrier, len(friends))

    counter = [0]
    pending = []

    def take(n):
        at = counter[0]
        counter[0] += n
        assert counter[0] <= N_SEMS
        return at

    def remote(src, dst, sem, to):
        return pltpu.make_async_remote_copy(
            src_ref=src, dst_ref=dst, send_sem=ss.at[sem], recv_sem=rs.at[sem],
            device_id=to, device_id_type=MESH,
        )

    def send(src, dst, sem, to):
        copy = remote(src, dst, sem, to)
        copy.start()
        pending.append(copy)
        return copy

    class Line:
        def __init__(self, own, slots):
            self.own, self.slots, self.sem = own, slots, take(8)

        def hop(self, s, way, own=False):
            src = self.own if own else self.slots.at[s]
            return pltpu.make_async_remote_copy(
                src_ref=src, dst_ref=self.slots.at[s],
                send_sem=ss.at[self.sem + 4 * way + s], recv_sem=rs.at[self.sem + s],
                device_id=left if way else right, device_id_type=MESH,
            )

        def begin(self):
            @pl.when(z < 3)
            def _():
                self.hop(z, 0, True).start()

            @pl.when(z > 0)
            def _():
                self.hop(z, 1, True).start()

        def step(self, distance):
            @pl.when(z - distance >= 0)
            def _():
                self.hop(z - distance, 0).wait_recv()

                @pl.when(z < 3)
                def _():
                    self.hop(z - distance, 0).start()

            @pl.when(z + distance <= 3)
            def _():
                self.hop(z + distance, 1).wait_recv()

                @pl.when(z > 0)
                def _():
                    self.hop(z + distance, 1).start()

        def finish(self):
            for distance in range(4):
                @pl.when((z - distance >= 0) & (z < 3))
                def _():
                    self.hop(z - distance, 0, distance == 0).wait_send()

                @pl.when((z + distance <= 3) & (z > 0))
                def _():
                    self.hop(z + distance, 1, distance == 0).wait_send()

    line_x = Line(x_ref, gx)
    line_c = Line(c_ref, gc)
    line_x.begin()

    half = pl.ds(2 * c, 2)
    e_in = [send(e_ref.at[half, turn(x, k)], eb.at[x, half], take(1), xp[k]) for k in (1, 3, 2)]
    local_e = pltpu.make_async_copy(e_ref.at[:, x], eb.at[x], ls.at[0])
    local_w = pltpu.make_async_copy(w_ref.at[:, x], wb.at[x], ls.at[1])
    local_e.start()
    local_w.start()

    wide = x_ref[...].astype(F32)
    stat_x[0] = jnp.broadcast_to(jnp.sum(wide * wide, axis=0, keepdims=True), (8, tok))
    stat_a = [send(stat_x.at[0], stat_x.at[k], take(1), xp[k]) for k in (1, 2, 3)]
    gx[z] = x_ref[...]
    gc[z] = c_ref[...]
    for copy in stat_a:
        copy.wait_recv()
    stat_z[0] = stat_x[0] + stat_x[1] + stat_x[2] + stat_x[3]
    stat_b = [send(stat_z.at[0], stat_z.at[k], take(1), zp[k]) for k in (1, 2, 3)]

    local_e.wait()

    def turn_e(block):
        for j in range(4):
            ebt[block, :, j * chunk : (j + 1) * chunk] = jnp.transpose(
                eb[block, j].astype(F32)
            ).astype(BF16)

    def turn_w(block):
        for j in range(4):
            wbt[block, :, j * sub : (j + 1) * sub] = jnp.transpose(
                wb[block, j].astype(F32)
            ).astype(BF16)

    turn_e(x)
    line_x.step(1)
    e_fwd = []
    for copy, k in zip(e_in, (1, 3, 2)):
        copy.wait_recv()
        at = turn(x, -k)
        e_fwd.append(send(eb.at[at, half], eb.at[at, half], take(1), cp))
    w_in = [send(w_ref.at[half, turn(x, k)], wb.at[x, half], take(1), xp[k]) for k in (1, 3, 2)]
    line_x.step(2)
    line_c.begin()
    for copy, k in zip(e_fwd, (1, 3, 2)):
        copy.wait_recv()
        turn_e(turn(x, -k))
    for copy in stat_b:
        copy.wait_recv()
    total = stat_z[0] + stat_z[1] + stat_z[2] + stat_z[3]
    scale = lax.rsqrt(total[0:1] * (1.0 / features) + 1e-05)
    line_x.step(3)
    for j in range(4):
        rows = slice(j * chunk, (j + 1) * chunk)
        normed[rows] = (gx[j].astype(F32) * scale * gain_ref[rows]).astype(BF16)

    def scatter(make, out, landed, to):
        copies = []
        for k in (2, 1, 3):
            out[k] = make(k).astype(BF16)
            copies.append(send(out.at[k], landed.at[k], take(1), to[k]))
        acc[...] = make(0)
        return copies

    def collect(copies, landed):
        total = acc[...]
        for copy, k in zip(copies, (2, 1, 3)):
            copy.wait_recv()
            total = total + landed[k].astype(F32)
        return total

    def share(slots, value, to):
        slots[x] = value.astype(BF16)
        return [send(slots.at[x], slots.at[x], take(1), to[k]) for k in (2, 1, 3)]

    def arrive(copies):
        for copy in copies:
            copy.wait_recv()

    r_copies = scatter(lambda k: nn(ebt[turn(x, k)], normed[...]), r_s, r_r, xp)
    line_c.step(1)
    r_all = share(r_g, collect(r_copies, r_r), xp)
    local_w.wait()
    turn_w(x)
    w_fwd = []
    for copy, k in zip(w_in, (1, 3, 2)):
        copy.wait_recv()
        at = turn(x, -k)
        w_fwd.append(send(wb.at[at, half], wb.at[at, half], take(1), cp))
    line_c.step(2)
    for copy, k in zip(w_fwd, (1, 3, 2)):
        copy.wait_recv()
        turn_w(turn(x, -k))
    arrive(r_all)

    def p_part(k):
        at = turn(z, k)
        total = nn(wb[0, at], r_g[0])
        for j in range(1, 4):
            total = total + nn(wb[j, at], r_g[j])
        return total

    p_copies = scatter(p_part, p_s, p_r, zp)
    p_sum = acc[...]
    o_own[0:sub] = p_sum
    line_c.step(3)

    def b_part(k):
        total = nn(ebt[turn(x, k), :, 0:chunk], gc[0])
        for j in range(1, 4):
            total = total + nn(ebt[turn(x, k), :, j * chunk : (j + 1) * chunk], gc[j])
        return total

    b_copies = scatter(b_part, b_s, b_r, xp)
    b_g[z] = collect(b_copies, b_r).astype(BF16)
    line_b = Line(b_g.at[z], b_g)
    line_b.begin()

    acc[...] = o_own[0:sub]
    p_all = share(p_g, collect(p_copies, p_r), xp)
    line_b.step(1)
    line_b.step(2)
    arrive(p_all)
    line_b.step(3)

    def q_part(k):
        at = turn(x, k)
        total = nn(wbt[at, :, 0:sub], b_g[0])
        for j in range(1, 4):
            total = total + nn(wbt[at, :, j * sub : (j + 1) * sub], b_g[j])
        return total

    q_copies = scatter(q_part, q_s, q_r, xp)

    def o_part(k):
        at = turn(z, k)
        total = nn(eb[0, at], p_g[0])
        for j in range(1, 4):
            total = total + nn(eb[j, at], p_g[j])
        return total

    q_all = share(q_g, collect(q_copies, q_r), xp)

    o_copies = []
    for k in (2, 1, 3):
        o_s[k] = o_part(k).astype(BF16)
        o_copies.append(send(o_s.at[k], o_r.at[k], take(1), zp[k]))
    o_own[...] = o_part(0)

    order = (0, 2, 1, 3)
    for t, k in enumerate(order):
        for j in range(4):
            grad[t, j * chunk : (j + 1) * chunk] = nt(gc[j], p_g[turn(x, -k)])

    halves = 2 * chunk
    quarter, eighth = halves // 4, halves // 8
    stage = {}

    def grad_block(t):
        at = turn(x, -order[t])
        if t:
            q_all[t - 1].wait_recv()
        back = q_g[at]
        away = pl.ds(pl.multiple_of((1 - c) * halves, halves), halves)
        home = pl.ds(pl.multiple_of(c * halves, halves), halves)
        gs[t] = (grad[t, away] + nt(normed[away], back)).astype(BF16)
        stage["c", t] = send(gs.at[t], gr.at[t], take(1), cp)
        grad[t, home] = grad[t, home] + nt(normed[home], back)

    def over_y(t):
        stage["c", t].wait_recv()
        copies = []
        for k in (2, 1, 3, 0):
            at = turn(y, k) * quarter
            mine = pl.ds(pl.multiple_of(c * halves + at, quarter), quarter)
            theirs = pl.ds(pl.multiple_of(at, quarter), quarter)
            total = grad[t, mine] + gr[t, theirs].astype(F32)
            if k:
                ys[t, k] = total.astype(BF16)
                copies.append(send(ys.at[t, k], yr.at[t, k], take(1), yp[k]))
            else:
                y_own[t] = total
        stage["y", t] = copies

    def over_h(t):
        arrive(stage["y", t])
        def part(at):
            rows = pl.ds(pl.multiple_of(at * eighth, eighth), eighth)
            total = y_own[t, rows]
            for k in (1, 2, 3):
                total = total + yr[t, k, rows].astype(F32)
            return total
        zs[t] = part(1 - h).astype(BF16)
        stage["h", t] = send(zs.at[t], zr.at[t], take(1), hp)
        z_own[t] = part(h)

    piece = c * 8 + y * 2 + h

    def over_x(t):
        stage["h", t].wait_recv()
        total = (z_own[t] + zr[t].astype(F32)).astype(BF16)
        k = order[t]
        if k:
            x_s[t] = total
            stage["x", t] = send(x_s.at[t], fg.at[piece, x], take(1), xp[(4 - k) % 4])
        else:
            fg[piece, x] = total

    grad_block(0)
    grad_block(1)
    over_y(0)
    grad_block(2)
    over_y(1)
    over_h(0)
    grad_block(3)
    over_y(2)
    over_h(1)
    over_x(0)
    over_y(3)
    over_h(2)
    over_x(1)
    over_h(3)
    over_x(2)
    over_x(3)

    total = x_ref[...].astype(F32) + o_own[...]
    for copy, k in zip(o_copies, (2, 1, 3)):
        copy.wait_recv()
        total = total + o_r[k].astype(F32)
    mixed_ref[...] = total.astype(BF16)

    for t in (1, 2, 3):
        stage["x", t].wait_recv()

    def give(at, to):
        return send(fg.at[at], fg.at[at], take(1), to)

    from_h = give(piece, hp)
    from_y0 = [give(piece, yp[k]) for k in (2, 1, 3)]
    from_c = [give(piece, cp)]
    from_h.wait_recv()
    other = c * 8 + y * 2 + (1 - h)
    from_y1 = [give(other, yp[k]) for k in (2, 1, 3)]
    from_c.append(give(other, cp))
    for copies, at_h in ((from_y0, h), (from_y1, 1 - h)):
        for copy, k in zip(copies, (2, 1, 3)):
            copy.wait_recv()
            from_c.append(give(c * 8 + turn(y, -k) * 2 + at_h, cp))
    arrive(from_c)

    line_x.finish()
    line_c.finish()
    line_b.finish()
    for copy in pending:
        copy.wait_send()


def per_device(tokens, norm_gain, expansion, small_weight, cotangent):
    tok, chunk = tokens.shape
    sub = expansion.shape[1]
    x = lax.axis_index("fsdp") % 4
    gain = lax.dynamic_index_in_dim(norm_gain.reshape(4, 4, chunk), x, 1, False)
    gain = gain.reshape(4 * chunk, 1)
    half, eighth = 2 * chunk, chunk // 4
    quarter = half // 4

    def v(*shape, dtype=BF16):
        return pltpu.VMEM(shape, dtype)

    trio = [v(4, sub, tok)] * 3
    mixed, pieces = pl.pallas_call(
        kernel,
        out_shape=[
            jax.ShapeDtypeStruct((chunk, tok), BF16),
            jax.ShapeDtypeStruct((16, 4, eighth, sub), BF16),
        ],
        in_specs=[
            pl.BlockSpec(memory_space=pltpu.VMEM),
            pl.BlockSpec(memory_space=pltpu.VMEM),
            pl.BlockSpec(memory_space=pl.ANY),
            pl.BlockSpec(memory_space=pl.ANY),
            pl.BlockSpec(memory_space=pltpu.VMEM),
        ],
        out_specs=[pl.BlockSpec(memory_space=pltpu.VMEM)] * 2,
        scratch_shapes=[
            v(4, 8, tok, dtype=F32), v(4, 8, tok, dtype=F32),
            v(4, chunk, tok), v(4, chunk, tok), v(4 * chunk, tok),
            v(4, 4, chunk, sub), v(4, sub, 4 * chunk),
            v(4, 4, sub, sub), v(4, sub, 4 * sub),
            *trio, *trio, *trio, *trio,
            v(4, chunk, tok), v(4, chunk, tok), v(sub, tok, dtype=F32), v(chunk, tok, dtype=F32),
            v(4, 4 * chunk, sub, dtype=F32),
            v(4, half, sub), v(4, half, sub),
            v(4, 4, quarter, sub), v(4, 4, quarter, sub),
            v(4, eighth, sub), v(4, eighth, sub),
            v(4, quarter, sub, dtype=F32), v(4, eighth, sub, dtype=F32), v(4, eighth, sub),
            pltpu.SemaphoreType.DMA((N_SEMS,)),
            pltpu.SemaphoreType.DMA((N_SEMS,)),
            pltpu.SemaphoreType.DMA((2,)),
        ],
        compiler_params=pltpu.CompilerParams(
            collective_id=0, has_side_effects=True, vmem_limit_bytes=60 * 1024 * 1024
        ),
        name="width_growth",
    )(
        tokens.T,
        gain,
        expansion.reshape(4, 4, chunk, sub),
        small_weight.reshape(4, 4, sub, sub),
        cotangent.T,
    )
    grad = pieces.reshape(4, 4, 4, eighth, sub).transpose(0, 2, 1, 3, 4)
    return mixed.T, grad.reshape(16 * chunk, sub).astype(F32)


def solution(mesh):
    in_specs = (P("dp", "fsdp"), P(), P(None, "fsdp"), P(None, "fsdp"), P("dp", "fsdp"))
    out_specs = (P("dp", "fsdp"), P(None, "fsdp"))
    return jax.shard_map(
        per_device, mesh=mesh, in_specs=in_specs, out_specs=out_specs, check_vma=False
    )
```

```python
import jax
import jax.numpy as jnp
from jax import lax
from jax.experimental import pallas as pl
from jax.experimental.pallas import tpu as pltpu
from jax.sharding import PartitionSpec as P

MESH = pl.DeviceIdType.MESH
F32 = jnp.float32
BF16 = jnp.bfloat16
N_SEMS = 192
HALVES = 2


def nn(a, b):
    return lax.dot_general(a, b, (((1,), (0,)), ((), ())), preferred_element_type=F32)


def nt(a, b):
    return lax.dot_general(a, b, (((1,), (1,)), ((), ())), preferred_element_type=F32)


def kernel(
    x_ref, gain_ref, e_ref, w_ref, c_ref, mixed_ref, fg,
    stat_x, stat_z, gain, gx, gc, normed, eb, ebt, wb, wbt,
    r_s, r_r, r_g, p_s, p_r, p_g, b_s, b_r, b_g, q_s, q_r, q_g,
    o_s, o_r, own, o_own, grad, gs, gr, ys, yr, zs, zr, y_own, z_own, x_s,
    ss, rs, ls,
):
    chunk, tok = x_ref.shape
    part = tok // HALVES
    sub = w_ref.shape[2]
    features = chunk * 16
    d, f = lax.axis_index("dp"), lax.axis_index("fsdp")
    y, h, c = d // 4, (d // 2) % 2, d % 2
    z, x = f // 4, f % 4

    def dev(y=y, h=h, c=c, z=z, x=x):
        return {"dp": y * 4 + h * 2 + c, "fsdp": z * 4 + x}

    def turn(v, k):
        return lax.rem(v + k + 4, 4)

    xp = [dev(x=turn(x, k)) for k in range(4)]
    zp = [dev(z=turn(z, k)) for k in range(4)]
    yp = [dev(y=turn(y, k)) for k in range(4)]
    hp, cp = dev(h=1 - h), dev(c=1 - c)

    barrier = pltpu.get_barrier_semaphore()
    friends = xp[1:] + zp[1:] + yp[1:] + [hp, cp]
    for friend in friends:
        pl.semaphore_signal(barrier, inc=1, device_id=friend, device_id_type=MESH)
    pl.semaphore_wait(barrier, len(friends))

    counter = [0]
    pending = []
    lines = []

    def take(n):
        at = counter[0]
        counter[0] += n
        assert counter[0] <= N_SEMS
        return at

    def remote(src, dst, send_sem, recv_sem, to):
        return pltpu.make_async_remote_copy(
            src_ref=src, dst_ref=dst, send_sem=ss.at[send_sem], recv_sem=rs.at[recv_sem],
            device_id=to, device_id_type=MESH,
        )

    def send(src, dst, to):
        sem = take(1)
        copy = remote(src, dst, sem, sem, to)
        copy.start()
        pending.append(copy)
        return copy

    def arrive(copies):
        for copy in copies:
            copy.wait_recv()

    class Line:
        def __init__(self, own, slots):
            self.own, self.slots, self.sem = own, slots, take(5)
            lines.append(self)

        def sends(self):
            for way, (ok, to) in enumerate((
                (z < 3, z + 1), (z > 0, z - 1), (z < 2, z + 2), (z > 1, z - 2),
            )):
                to = jnp.clip(to, 0, 3)
                yield ok, remote(
                    self.own, self.slots.at[z], self.sem + way, self.sem + z, dev(z=to)
                )

        def handed(self):
            at = jnp.clip(3 * (2 - z), 0, 3)
            to = jnp.clip(3 * (z - 1), 0, 3)
            return at, remote(
                self.slots.at[at], self.slots.at[at], self.sem + 4, self.sem + at, dev(z=to)
            )

        def begin(self):
            for ok, copy in self.sends():
                @pl.when(ok)
                def _():
                    copy.start()

        def hand_over(self):
            @pl.when((z == 1) | (z == 2))
            def _():
                at, copy = self.handed()
                copy.wait_recv()
                copy.start()

        def arrive(self):
            for s in range(4):
                ok = z != s
                if s == 0:
                    ok = ok & (z != 2)
                if s == 3:
                    ok = ok & (z != 1)

                @pl.when(ok)
                def _():
                    block = self.slots.at[s]
                    remote(block, block, self.sem, self.sem + s, dev(z=turn(z, 1))).wait_recv()

        def finish(self):
            for ok, copy in self.sends():
                @pl.when(ok)
                def _():
                    copy.wait_send()

            @pl.when((z == 1) | (z == 2))
            def _():
                self.handed()[1].wait_send()

    both = range(HALVES)

    def cut(ref, i):
        return ref.at[:, pl.ds(i * part, part)]

    line_x = [Line(cut(x_ref, i), gx.at[i]) for i in both]
    line_c = [Line(cut(c_ref, i), gc.at[i]) for i in both]
    line_x[0].begin()

    half = pl.ds(2 * c, 2)
    e_in = [send(e_ref.at[half, turn(x, k)], eb.at[x, half], xp[k]) for k in (1, 3, 2)]
    local_e = pltpu.make_async_copy(e_ref.at[:, x], eb.at[x], ls.at[0])
    local_w = pltpu.make_async_copy(w_ref.at[:, x], wb.at[x], ls.at[1])
    local_e.start()
    local_w.start()

    wide = x_ref[...].astype(F32)
    stat_x[0] = jnp.broadcast_to(jnp.sum(wide * wide, axis=0, keepdims=True), (8, tok))
    stat_a = [send(stat_x.at[0], stat_x.at[k], xp[k]) for k in (1, 2, 3)]
    for i in both[1:]:
        line_x[i].begin()
    for i in both:
        gx[i, z] = x_ref[:, i * part : (i + 1) * part]
        gc[i, z] = c_ref[:, i * part : (i + 1) * part]
    rows = lax.broadcasted_iota(jnp.int32, (chunk, chunk), 0)
    cols = lax.broadcasted_iota(jnp.int32, (chunk, chunk), 1)
    for j in range(4):
        line = gain_ref[pl.ds(j * 4 + x, 1)]
        gain[j] = jnp.sum(jnp.where(rows == cols, line, 0.0), axis=1, keepdims=True)
    arrive(stat_a)
    stat_z[0] = stat_x[0] + stat_x[1] + stat_x[2] + stat_x[3]
    stat_b = [send(stat_z.at[0], stat_z.at[k], zp[k]) for k in (1, 2, 3)]

    def turn_e(block):
        ebt[block] = jnp.transpose(eb[block].reshape(4 * chunk, sub))

    def turn_w(block):
        wbt[block] = jnp.transpose(wb[block].reshape(4 * sub, sub))

    local_e.wait()
    turn_e(x)
    line_x[0].hand_over()
    e_fwd = []
    for copy, k in zip(e_in, (1, 3, 2)):
        copy.wait_recv()
        at = turn(x, -k)
        e_fwd.append(send(eb.at[at, half], eb.at[at, half], cp))
    w_in = [send(w_ref.at[half, turn(x, k)], wb.at[x, half], xp[k]) for k in (1, 3, 2)]
    line_x[0].arrive()
    line_c[0].begin()
    arrive(stat_b)
    total = stat_z[0] + stat_z[1] + stat_z[2] + stat_z[3]
    scale = lax.rsqrt(total[0:1] * (1.0 / features) + 1e-05)

    def norm(i):
        for j in range(4):
            wide = gx[i, j].astype(F32) * scale[:, i * part : (i + 1) * part] * gain[j]
            normed[i, j * chunk : (j + 1) * chunk] = wide.astype(BF16)

    norm(0)
    for copy, k in zip(e_fwd, (1, 3, 2)):
        copy.wait_recv()
        turn_e(turn(x, -k))

    def scatter(make, out, landed, mine, to):
        copies = []
        for k in (2, 1, 3):
            out[k] = make(k).astype(BF16)
            copies.append(send(out.at[k], landed.at[k], to[k]))
        mine[...] = make(0)
        return copies

    def collect(copies, landed, mine):
        total = mine[...]
        for copy, k in zip(copies, (2, 1, 3)):
            copy.wait_recv()
            total = total + landed[k].astype(F32)
        return total

    def share(slots, value):
        slots[x] = value.astype(BF16)
        return [send(slots.at[x], slots.at[x], xp[k]) for k in (2, 1, 3)]

    def stacked(block):
        return block.reshape(block.shape[0] * block.shape[1], block.shape[2])

    def scatter_r(i):
        return scatter(
            lambda k: nn(ebt[turn(x, k)], normed[i]), r_s.at[i], r_r.at[i], own.at[0, i], xp
        )

    def scatter_p(i):
        def make(k):
            at = turn(z, k)
            total = nn(wb[0, at], r_g[i, 0])
            for j in range(1, 4):
                total = total + nn(wb[j, at], r_g[i, j])
            return total

        return scatter(make, p_s.at[i], p_r.at[i], own.at[1, i], zp)

    def scatter_b(i):
        return scatter(
            lambda k: nn(ebt[turn(x, k)], stacked(gc[i])),
            b_s.at[i], b_r.at[i], own.at[2, i], xp,
        )

    def scatter_q(i):
        return scatter(
            lambda k: nn(wbt[turn(x, k)], stacked(b_g[i])),
            q_s.at[i], q_r.at[i], own.at[3, i], xp,
        )

    def scatter_o(i):
        def make(k):
            at = turn(z, k)
            total = nn(eb[0, at], p_g[i, 0])
            for j in range(1, 4):
                total = total + nn(eb[j, at], p_g[i, j])
            return total

        return scatter(make, o_s.at[i], o_r.at[i], o_own.at[i], zp)

    r_sum, r_all, p_sum, p_all = {}, {}, {}, {}
    b_sum, q_sum, q_all, o_sum = {}, {}, {}, {}
    r_sum[0] = scatter_r(0)
    line_x[1].hand_over()
    line_x[1].arrive()
    line_c[1].begin()
    norm(1)
    r_sum[1] = scatter_r(1)
    line_c[0].hand_over()
    r_all[0] = share(r_g.at[0], collect(r_sum[0], r_r.at[0], own.at[0, 0]))
    local_w.wait()
    w_fwd = []
    for copy, k in zip(w_in, (1, 3, 2)):
        copy.wait_recv()
        at = turn(x, -k)
        w_fwd.append(send(wb.at[at, half], wb.at[at, half], cp))
    r_all[1] = share(r_g.at[1], collect(r_sum[1], r_r.at[1], own.at[0, 1]))
    line_c[0].arrive()
    arrive(w_fwd)

    arrive(r_all[0])
    p_sum[0] = scatter_p(0)
    b_sum[0] = scatter_b(0)
    line_c[1].hand_over()
    arrive(r_all[1])
    p_sum[1] = scatter_p(1)
    line_c[1].arrive()
    b_sum[1] = scatter_b(1)

    line_b = [Line(b_g.at[i, z], b_g.at[i]) for i in both]

    def gather_b(i):
        b_g[i, z] = collect(b_sum[i], b_r.at[i], own.at[2, i]).astype(BF16)
        line_b[i].begin()

    gather_b(0)
    p_all[0] = share(p_g.at[0], collect(p_sum[0], p_r.at[0], own.at[1, 0]))
    line_b[0].hand_over()
    gather_b(1)
    p_all[1] = share(p_g.at[1], collect(p_sum[1], p_r.at[1], own.at[1, 1]))
    for j in range(4):
        turn_w(j)

    line_b[0].arrive()
    q_sum[0] = scatter_q(0)
    line_b[1].hand_over()
    arrive(p_all[0])
    order = (0, 2, 1, 3)

    def cotangent_part(i, t):
        at = turn(x, -order[t])
        for j in range(4):
            rows = slice(j * chunk, (j + 1) * chunk)
            product = nt(gc[i, j], p_g[i, at])
            grad[t, rows] = product if i == 0 else grad[t, rows] + product

    line_b[1].arrive()
    q_sum[1] = scatter_q(1)
    q_all[0] = share(q_g.at[0], collect(q_sum[0], q_r.at[0], own.at[3, 0]))
    o_sum[0] = scatter_o(0)
    arrive(p_all[1])
    q_all[1] = share(q_g.at[1], collect(q_sum[1], q_r.at[1], own.at[3, 1]))
    o_sum[1] = scatter_o(1)
    for t in range(4):
        for i in both:
            cotangent_part(i, t)

    halves = 2 * chunk
    quarter, eighth = halves // 4, halves // 8
    stage = {}

    def grad_block(t):
        at = turn(x, -order[t])
        if t:
            for i in both:
                q_all[i][t - 1].wait_recv()
        away = pl.ds(pl.multiple_of((1 - c) * halves, halves), halves)
        home = pl.ds(pl.multiple_of(c * halves, halves), halves)

        def total(rows):
            value = grad[t, rows]
            for i in both:
                value = value + nt(normed[i, rows], q_g[i, at])
            return value

        gs[t] = total(away).astype(BF16)
        stage["c", t] = send(gs.at[t], gr.at[t], cp)
        grad[t, home] = total(home)

    def over_y(t):
        stage["c", t].wait_recv()
        copies = []
        for k in (2, 1, 3, 0):
            at = turn(y, k) * quarter
            mine = pl.ds(pl.multiple_of(c * halves + at, quarter), quarter)
            theirs = pl.ds(pl.multiple_of(at, quarter), quarter)
            total = grad[t, mine] + gr[t, theirs].astype(F32)
            if k:
                ys[t, k] = total.astype(BF16)
                copies.append(send(ys.at[t, k], yr.at[t, k], yp[k]))
            else:
                y_own[t] = total
        stage["y", t] = copies

    def over_h(t):
        arrive(stage["y", t])

        def share_of(at):
            rows = pl.ds(pl.multiple_of(at * eighth, eighth), eighth)
            total = y_own[t, rows]
            for k in (1, 2, 3):
                total = total + yr[t, k, rows].astype(F32)
            return total

        zs[t] = share_of(1 - h).astype(BF16)
        stage["h", t] = send(zs.at[t], zr.at[t], hp)
        z_own[t] = share_of(h)

    def piece(c, y, h):
        return c * 2 + y // 2, (y % 2) * 2 + h

    first, last = piece(c, y, h)

    def over_x(t):
        stage["h", t].wait_recv()
        total = (z_own[t] + zr[t].astype(F32)).astype(BF16)
        k = order[t]
        if k:
            x_s[t] = total
            stage["x", t] = send(x_s.at[t], fg.at[first, x, last], xp[(4 - k) % 4])
        else:
            fg[first, x, last] = total

    grad_block(0)
    grad_block(1)
    over_y(0)
    grad_block(2)
    over_y(1)
    over_h(0)
    grad_block(3)
    over_y(2)
    over_h(1)
    over_x(0)
    over_y(3)
    over_h(2)
    over_x(1)
    over_h(3)
    over_x(2)
    over_x(3)

    for t in (1, 2, 3):
        stage["x", t].wait_recv()

    def give(at, to):
        return send(fg.at[at[0], :, at[1]], fg.at[at[0], :, at[1]], to)

    from_h = give(piece(c, y, h), hp)
    from_y0 = [give(piece(c, y, h), yp[k]) for k in (2, 1, 3)]
    from_c = [give(piece(c, y, h), cp)]
    from_h.wait_recv()
    from_y1 = [give(piece(c, y, 1 - h), yp[k]) for k in (2, 1, 3)]
    from_c.append(give(piece(c, y, 1 - h), cp))
    for copies, at_h in ((from_y0, h), (from_y1, 1 - h)):
        for copy, k in zip(copies, (2, 1, 3)):
            copy.wait_recv()
            from_c.append(give(piece(c, turn(y, -k), at_h), cp))

    for i in both:
        total = x_ref[:, i * part : (i + 1) * part].astype(F32)
        mixed_ref[:, i * part : (i + 1) * part] = (
            total + collect(o_sum[i], o_r.at[i], o_own.at[i])
        ).astype(BF16)
    arrive(from_c)

    for line in lines:
        line.finish()
    for copy in pending:
        copy.wait_send()


def per_device(tokens, norm_gain, expansion, small_weight, cotangent):
    tok, chunk = tokens.shape
    sub = expansion.shape[1]
    half, eighth = 2 * chunk, chunk // 4
    quarter, part = half // 4, tok // HALVES

    def v(*shape, dtype=BF16):
        return pltpu.VMEM(shape, dtype)

    trio = [v(HALVES, 4, sub, part)] * 3
    mixed, pieces = pl.pallas_call(
        kernel,
        out_shape=[
            jax.ShapeDtypeStruct((chunk, tok), BF16),
            jax.ShapeDtypeStruct((4, 4, 4, eighth, sub), BF16),
        ],
        in_specs=[
            pl.BlockSpec(memory_space=pltpu.VMEM),
            pl.BlockSpec(memory_space=pltpu.VMEM),
            pl.BlockSpec(memory_space=pl.ANY),
            pl.BlockSpec(memory_space=pl.ANY),
            pl.BlockSpec(memory_space=pltpu.VMEM),
        ],
        out_specs=[pl.BlockSpec(memory_space=pltpu.VMEM)] * 2,
        scratch_shapes=[
            v(4, 8, tok, dtype=F32), v(4, 8, tok, dtype=F32), v(4, chunk, 1, dtype=F32),
            v(HALVES, 4, chunk, part), v(HALVES, 4, chunk, part), v(HALVES, 4 * chunk, part),
            v(4, 4, chunk, sub), v(4, sub, 4 * chunk),
            v(4, 4, sub, sub), v(4, sub, 4 * sub),
            *trio, *trio, *trio, *trio,
            v(HALVES, 4, chunk, part), v(HALVES, 4, chunk, part),
            v(4, HALVES, sub, part, dtype=F32), v(HALVES, chunk, part, dtype=F32),
            v(4, 4 * chunk, sub, dtype=F32),
            v(4, half, sub), v(4, half, sub),
            v(4, 4, quarter, sub), v(4, 4, quarter, sub),
            v(4, eighth, sub), v(4, eighth, sub),
            v(4, quarter, sub, dtype=F32), v(4, eighth, sub, dtype=F32), v(4, eighth, sub),
            pltpu.SemaphoreType.DMA((N_SEMS,)),
            pltpu.SemaphoreType.DMA((N_SEMS,)),
            pltpu.SemaphoreType.DMA((2,)),
        ],
        compiler_params=pltpu.CompilerParams(
            collective_id=0, has_side_effects=True, vmem_limit_bytes=60 * 1024 * 1024
        ),
        name="width_growth",
    )(
        tokens.T,
        norm_gain.reshape(16, chunk),
        expansion.reshape(4, 4, chunk, sub),
        small_weight.reshape(4, 4, sub, sub),
        cotangent.T,
    )
    return mixed.T, pieces.reshape(16 * chunk, sub).astype(F32)


def solution(mesh):
    in_specs = (P("dp", "fsdp"), P(), P(None, "fsdp"), P(None, "fsdp"), P("dp", "fsdp"))
    out_specs = (P("dp", "fsdp"), P(None, "fsdp"))
    return jax.shard_map(
        per_device, mesh=mesh, in_specs=in_specs, out_specs=out_specs, check_vma=False
    )
```

```python
import jax
import jax.numpy as jnp
from jax import lax
from jax.experimental import pallas as pl
from jax.experimental.pallas import tpu as pltpu
from jax.sharding import PartitionSpec as P

MESH = pl.DeviceIdType.MESH
F32 = jnp.float32
BF16 = jnp.bfloat16
N_SEMS = 256
HALVES = 2


def nn(a, b):
    return lax.dot_general(a, b, (((1,), (0,)), ((), ())), preferred_element_type=F32)


def nt(a, b):
    return lax.dot_general(a, b, (((1,), (1,)), ((), ())), preferred_element_type=F32)


def kernel(
    x_ref, gain_ref, e_ref, w_ref, c_ref, mixed_ref, fg,
    stat_x, stat_z, gain, gx, gc, normed, eb, ebt, wb, wbt,
    r_s, r_r, r_g, p_s, p_r, p_g, b_s, b_r, b_g, q_s, q_r, q_g,
    o_s, o_r, p_h, o_h, own, o_own, grad, gs, gr, ys, yr, zs, zr, y_own, z_own, x_s,
    ss, rs, ls,
):
    chunk, tok = x_ref.shape
    part = tok // HALVES
    sub = w_ref.shape[2]
    features = chunk * 16
    d, f = lax.axis_index("dp"), lax.axis_index("fsdp")
    y, h, c = d // 4, (d // 2) % 2, d % 2
    z, x = f // 4, f % 4

    def dev(y=y, h=h, c=c, z=z, x=x):
        return {"dp": y * 4 + h * 2 + c, "fsdp": z * 4 + x}

    def turn(v, k):
        return lax.rem(v + k + 4, 4)

    xp = [dev(x=turn(x, k)) for k in range(4)]
    zp = [dev(z=turn(z, k)) for k in range(4)]
    yp = [dev(y=turn(y, k)) for k in range(4)]
    hp, cp = dev(h=1 - h), dev(c=1 - c)

    barrier = pltpu.get_barrier_semaphore()
    xhp = [dev(x=turn(x, k), h=1 - h) for k in range(4)]
    friends = xp[1:] + zp[1:] + yp[1:] + xhp + [cp]
    for friend in friends:
        pl.semaphore_signal(barrier, inc=1, device_id=friend, device_id_type=MESH)
    pl.semaphore_wait(barrier, len(friends))

    counter = [0]
    pending = []
    lines = []

    def take(n):
        at = counter[0]
        counter[0] += n
        assert counter[0] <= N_SEMS
        return at

    def remote(src, dst, send_sem, recv_sem, to):
        return pltpu.make_async_remote_copy(
            src_ref=src, dst_ref=dst, send_sem=ss.at[send_sem], recv_sem=rs.at[recv_sem],
            device_id=to, device_id_type=MESH,
        )

    def send(src, dst, to):
        sem = take(1)
        copy = remote(src, dst, sem, sem, to)
        copy.start()
        pending.append(copy)
        return copy

    def arrive(copies):
        for copy in copies:
            copy.wait_recv()

    class Line:
        def __init__(self, own, slots):
            self.own, self.slots, self.sem = own, slots, take(5)
            lines.append(self)

        def sends(self):
            for way, (ok, to) in enumerate((
                (z < 3, z + 1), (z > 0, z - 1), (z < 2, z + 2), (z > 1, z - 2),
            )):
                to = jnp.clip(to, 0, 3)
                yield ok, remote(
                    self.own, self.slots.at[z], self.sem + way, self.sem + z, dev(z=to)
                )

        def handed(self):
            at = jnp.clip(3 * (2 - z), 0, 3)
            to = jnp.clip(3 * (z - 1), 0, 3)
            return at, remote(
                self.slots.at[at], self.slots.at[at], self.sem + 4, self.sem + at, dev(z=to)
            )

        def begin(self):
            for ok, copy in self.sends():
                @pl.when(ok)
                def _():
                    copy.start()

        def hand_over(self):
            @pl.when((z == 1) | (z == 2))
            def _():
                at, copy = self.handed()
                copy.wait_recv()
                copy.start()

        def arrive(self):
            for s in range(4):
                ok = z != s
                if s == 0:
                    ok = ok & (z != 2)
                if s == 3:
                    ok = ok & (z != 1)

                @pl.when(ok)
                def _():
                    block = self.slots.at[s]
                    remote(block, block, self.sem, self.sem + s, dev(z=turn(z, 1))).wait_recv()

        def finish(self):
            for ok, copy in self.sends():
                @pl.when(ok)
                def _():
                    copy.wait_send()

            @pl.when((z == 1) | (z == 2))
            def _():
                self.handed()[1].wait_send()

    class LineSum:
        def __init__(self, make, out, landed, held, mine):
            self.out, self.landed, self.held, self.mine = out, landed, held, mine
            self.sem = take(5)
            lines.append(self)
            for k in (3, 1):
                out[k] = make(turn(z, k)).astype(BF16)
                self.copy(k).start()
            held[...] = make(turn(z, 2))

            @pl.when((z == 0) | (z == 3))
            def _():
                out[2] = held[...].astype(BF16)
                self.copy(2).start()

            mine[...] = make(z)

        def copy(self, k):
            if k == 3:
                to, slot = jnp.where(z > 0, z - 1, 1), jnp.where(z > 0, z, 4)
            elif k == 1:
                to, slot = jnp.where(z < 3, z + 1, 2), jnp.where(z < 3, z, 4)
            else:
                to, slot = turn(z, 2), z
            return remote(
                self.out.at[k], self.landed.at[slot], self.sem + k, self.sem + slot, dev(z=to)
            )

        def landing(self, s):
            block = self.landed.at[s]
            return remote(block, block, self.sem, self.sem + s, dev(z=turn(z, 1)))

        def hand_over(self):
            @pl.when((z == 1) | (z == 2))
            def _():
                self.landing(4).wait_recv()
                total = self.held[...] + self.landed[4].astype(F32)
                self.out[2] = total.astype(BF16)
                self.copy(2).start()

        def collect(self):
            for s in range(4):
                ok = z != s
                if s in (0, 3):
                    ok = ok & (z != 3 - s)

                @pl.when(ok)
                def _():
                    self.landing(s).wait_recv()
                    self.mine[...] = self.mine[...] + self.landed[s].astype(F32)

            return self.mine[...]

        def finish(self):
            for k in (1, 2, 3):
                self.copy(k).wait_send()

    both = range(HALVES)

    def cut(ref, i):
        return ref.at[:, pl.ds(i * part, part)]

    line_x = [Line(cut(x_ref, i), gx.at[i]) for i in both]
    line_c = [Line(cut(c_ref, i), gc.at[i]) for i in both]
    line_x[0].begin()

    half = pl.ds(2 * c, 2)
    e_in = [send(e_ref.at[half, turn(x, k)], eb.at[x, half], xp[k]) for k in (1, 3, 2)]
    local_e = pltpu.make_async_copy(e_ref.at[:, x], eb.at[x], ls.at[0])
    local_w = pltpu.make_async_copy(w_ref.at[:, x], wb.at[x], ls.at[1])
    local_e.start()
    local_w.start()

    wide = x_ref[...].astype(F32)
    stat_x[0] = jnp.broadcast_to(jnp.sum(wide * wide, axis=0, keepdims=True), (8, tok))
    stat_a = [send(stat_x.at[0], stat_x.at[k], xp[k]) for k in (1, 2, 3)]
    for i in both[1:]:
        line_x[i].begin()
    for i in both:
        gx[i, z] = x_ref[:, i * part : (i + 1) * part]
        gc[i, z] = c_ref[:, i * part : (i + 1) * part]
    rows = lax.broadcasted_iota(jnp.int32, (chunk, chunk), 0)
    cols = lax.broadcasted_iota(jnp.int32, (chunk, chunk), 1)
    for j in range(4):
        line = gain_ref[pl.ds(j * 4 + x, 1)]
        gain[j] = jnp.sum(jnp.where(rows == cols, line, 0.0), axis=1, keepdims=True)
    arrive(stat_a)
    stat_z[0] = stat_x[0] + stat_x[1] + stat_x[2] + stat_x[3]
    stat_b = [send(stat_z.at[0], stat_z.at[k], zp[k]) for k in (1, 2, 3)]

    def turn_e(block):
        ebt[block] = jnp.transpose(eb[block].reshape(4 * chunk, sub))

    def turn_w(block):
        wbt[block] = jnp.transpose(wb[block].reshape(4 * sub, sub))

    local_e.wait()
    turn_e(x)
    line_x[0].hand_over()
    e_fwd = []
    for copy, k in zip(e_in, (1, 3, 2)):
        copy.wait_recv()
        at = turn(x, -k)
        e_fwd.append(send(eb.at[at, half], eb.at[at, half], cp))
    w_in = [send(w_ref.at[half, turn(x, k)], wb.at[x, half], xp[k]) for k in (1, 3, 2)]
    line_x[0].arrive()
    line_c[0].begin()
    arrive(stat_b)
    total = stat_z[0] + stat_z[1] + stat_z[2] + stat_z[3]
    scale = lax.rsqrt(total[0:1] * (1.0 / features) + 1e-05)

    def norm(i):
        for j in range(4):
            wide = gx[i, j].astype(F32) * scale[:, i * part : (i + 1) * part] * gain[j]
            normed[i, j * chunk : (j + 1) * chunk] = wide.astype(BF16)

    norm(0)
    line_x[1].hand_over()
    for copy, k in zip(e_fwd, (1, 3, 2)):
        copy.wait_recv()
        turn_e(turn(x, -k))

    def scatter(make, out, landed, mine, to):
        copies = []
        for k in (2, 1, 3):
            out[k] = make(k).astype(BF16)
            copies.append(send(out.at[k], landed.at[k], to[k]))
        mine[...] = make(0)
        return copies

    def collect(copies, landed, mine):
        total = mine[...]
        for copy, k in zip(copies, (2, 1, 3)):
            copy.wait_recv()
            total = total + landed[k].astype(F32)
        return total

    def share(slots, value):
        slots[x] = value.astype(BF16)
        return [send(slots.at[x], slots.at[x], xp[k]) for k in (2, 1, 3)]

    def stacked(block):
        return block.reshape(block.shape[0] * block.shape[1], block.shape[2])

    def scatter_r(i):
        return scatter(
            lambda k: nn(ebt[turn(x, k)], normed[i]), r_s.at[i], r_r.at[i], own.at[0, i], xp
        )

    def scatter_p(i):
        def make(at):
            total = nn(wb[0, at], r_g[i, 0])
            for j in range(1, 4):
                total = total + nn(wb[j, at], r_g[i, j])
            return total

        return LineSum(make, p_s.at[i], p_r.at[i], p_h.at[i], own.at[1, i])

    def scatter_b(i):
        return scatter(
            lambda k: nn(ebt[turn(x, k)], stacked(gc[i])),
            b_s.at[i], b_r.at[i], own.at[2, i], xp,
        )

    def scatter_q(i):
        return scatter(
            lambda k: nn(wbt[turn(x, k)], stacked(b_g[i])),
            q_s.at[i], q_r.at[i], own.at[3, i], xp,
        )

    def scatter_o(i):
        def make(at):
            total = nn(eb[0, at], p_g[i, 0])
            for j in range(1, 4):
                total = total + nn(eb[j, at], p_g[i, j])
            return total

        return LineSum(make, o_s.at[i], o_r.at[i], o_h.at[i], o_own.at[i])

    r_sum, r_all, p_sum, p_all = {}, {}, {}, {}
    b_sum, q_sum, q_all, o_sum = {}, {}, {}, {}
    r_sum[0] = scatter_r(0)
    line_x[1].arrive()
    line_c[1].begin()
    norm(1)
    r_sum[1] = scatter_r(1)
    line_c[0].hand_over()
    r_all[0] = share(r_g.at[0], collect(r_sum[0], r_r.at[0], own.at[0, 0]))
    local_w.wait()
    w_fwd = []
    for copy, k in zip(w_in, (1, 3, 2)):
        copy.wait_recv()
        at = turn(x, -k)
        w_fwd.append(send(wb.at[at, half], wb.at[at, half], cp))
    r_all[1] = share(r_g.at[1], collect(r_sum[1], r_r.at[1], own.at[0, 1]))
    line_c[0].arrive()
    arrive(w_fwd)

    arrive(r_all[0])
    p_sum[0] = scatter_p(0)
    line_c[1].hand_over()
    b_sum[0] = scatter_b(0)
    p_sum[0].hand_over()
    arrive(r_all[1])
    p_sum[1] = scatter_p(1)
    line_c[1].arrive()
    b_sum[1] = scatter_b(1)

    line_b = [Line(b_g.at[i, z], b_g.at[i]) for i in both]

    def gather_b(i):
        b_g[i, z] = collect(b_sum[i], b_r.at[i], own.at[2, i]).astype(BF16)
        line_b[i].begin()

    gather_b(0)
    p_sum[1].hand_over()
    p_all[0] = share(p_g.at[0], p_sum[0].collect())
    line_b[0].hand_over()
    gather_b(1)
    p_all[1] = share(p_g.at[1], p_sum[1].collect())
    for j in range(4):
        turn_w(j)

    line_b[0].arrive()
    q_sum[0] = scatter_q(0)
    line_b[1].hand_over()
    arrive(p_all[0])
    order = (0, 2, 1, 3)

    def cotangent_part(i, t):
        at = turn(x, -order[t])
        for j in range(4):
            rows = slice(j * chunk, (j + 1) * chunk)
            product = nt(gc[i, j], p_g[i, at])
            grad[t, rows] = product if i == 0 else grad[t, rows] + product

    o_sum[0] = scatter_o(0)
    line_b[1].arrive()
    q_sum[1] = scatter_q(1)
    arrive(p_all[1])
    o_sum[1] = scatter_o(1)
    q_all[0] = share(q_g.at[0], collect(q_sum[0], q_r.at[0], own.at[3, 0]))
    for i in both:
        cotangent_part(i, 0)
    q_all[1] = share(q_g.at[1], collect(q_sum[1], q_r.at[1], own.at[3, 1]))

    halves = 2 * chunk
    quarter, eighth = halves // 4, halves // 8
    stage = {}

    def grad_block(t):
        at = turn(x, -order[t])
        if t:
            for i in both:
                q_all[i][t - 1].wait_recv()
        away = pl.ds(pl.multiple_of((1 - c) * halves, halves), halves)
        home = pl.ds(pl.multiple_of(c * halves, halves), halves)

        def total(rows):
            value = grad[t, rows]
            for i in both:
                value = value + nt(normed[i, rows], q_g[i, at])
            return value

        gs[t] = total(away).astype(BF16)
        stage["c", t] = send(gs.at[t], gr.at[t], cp)
        grad[t, home] = total(home)

    def over_y(t):
        stage["c", t].wait_recv()
        copies = []
        for k in (2, 1, 3, 0):
            at = turn(y, k) * quarter
            mine = pl.ds(pl.multiple_of(c * halves + at, quarter), quarter)
            theirs = pl.ds(pl.multiple_of(at, quarter), quarter)
            total = grad[t, mine] + gr[t, theirs].astype(F32)
            if k:
                ys[t, k] = total.astype(BF16)
                copies.append(send(ys.at[t, k], yr.at[t, k], yp[k]))
            else:
                y_own[t] = total
        stage["y", t] = copies

    def over_h(t):
        arrive(stage["y", t])

        def share_of(at):
            rows = pl.ds(pl.multiple_of(at * eighth, eighth), eighth)
            total = y_own[t, rows]
            for k in (1, 2, 3):
                total = total + yr[t, k, rows].astype(F32)
            return total

        zs[t] = share_of(1 - h).astype(BF16)
        stage["h", t] = send(zs.at[t], zr.at[t], hp)
        z_own[t] = share_of(h)

    def piece(c, y, h):
        return c * 2 + y // 2, (y % 2) * 2 + h

    first, last = piece(c, y, h)

    def over_x(t):
        stage["h", t].wait_recv()
        total = (z_own[t] + zr[t].astype(F32)).astype(BF16)
        k = order[t]
        if k:
            x_s[t] = total
            stage["x", t] = send(x_s.at[t], fg.at[first, x, last], xp[(4 - k) % 4])
            stage["xh", t] = send(x_s.at[t], fg.at[first, x, last], xhp[(4 - k) % 4])
        else:
            fg[first, x, last] = total
            slot = fg.at[first, x, last]
            stage["xh", t] = send(slot, slot, hp)

    given = {}

    def give(t, at, to):
        block = turn(x, order[t])
        return send(fg.at[at[0], block, at[1]], fg.at[at[0], block, at[1]], to)

    from_c = []

    def out_own(t):
        if t:
            stage["x", t].wait_recv()
        at = piece(c, y, h)
        given["y", t, 0] = [give(t, at, yp[k]) for k in (2, 1, 3)]
        from_c.append(give(t, at, cp))

    def out_other(t):
        stage["xh", t].wait_recv()
        at = piece(c, y, 1 - h)
        given["y", t, 1] = [give(t, at, yp[k]) for k in (2, 1, 3)]
        from_c.append(give(t, at, cp))

    def out_core(t, other):
        for copy, k in zip(given["y", t, other], (2, 1, 3)):
            copy.wait_recv()
            from_c.append(give(t, piece(c, turn(y, -k), 1 - h if other else h), cp))

    def finish_mixed():
        for i in both:
            total = x_ref[:, i * part : (i + 1) * part].astype(F32)
            mixed_ref[:, i * part : (i + 1) * part] = (
                total + o_sum[i].collect()
            ).astype(BF16)

    grad_block(0)
    o_sum[0].hand_over()
    over_y(0)
    for t in (1, 2):
        for i in both:
            cotangent_part(i, t)
    grad_block(1)
    o_sum[1].hand_over()
    over_h(0)
    for i in both:
        cotangent_part(i, 3)
    grad_block(2)
    over_y(1)
    grad_block(3)
    over_y(2)
    over_x(0)
    out_own(0)
    over_h(1)
    over_y(3)
    over_h(2)
    over_x(1)
    out_other(0)
    over_h(3)
    over_x(2)
    out_own(1)
    out_core(0, 0)
    over_x(3)
    out_own(2)
    out_other(1)
    out_core(0, 1)
    out_own(3)
    out_core(1, 0)
    out_other(2)
    out_core(1, 1)
    out_core(2, 0)
    out_other(3)
    finish_mixed()
    out_core(2, 1)
    out_core(3, 0)
    out_core(3, 1)
    arrive(from_c)

    for line in lines:
        line.finish()
    for copy in pending:
        copy.wait_send()


def per_device(tokens, norm_gain, expansion, small_weight, cotangent):
    tok, chunk = tokens.shape
    sub = expansion.shape[1]
    half, eighth = 2 * chunk, chunk // 4
    quarter, part = half // 4, tok // HALVES

    def v(*shape, dtype=BF16):
        return pltpu.VMEM(shape, dtype)

    trio = [v(HALVES, 4, sub, part)] * 3
    line_trio = [v(HALVES, 4, sub, part), v(HALVES, 5, sub, part), v(HALVES, 4, sub, part)]
    mixed, pieces = pl.pallas_call(
        kernel,
        out_shape=[
            jax.ShapeDtypeStruct((chunk, tok), BF16),
            jax.ShapeDtypeStruct((4, 4, 4, eighth, sub), BF16),
        ],
        in_specs=[
            pl.BlockSpec(memory_space=pltpu.VMEM),
            pl.BlockSpec(memory_space=pltpu.VMEM),
            pl.BlockSpec(memory_space=pl.ANY),
            pl.BlockSpec(memory_space=pl.ANY),
            pl.BlockSpec(memory_space=pltpu.VMEM),
        ],
        out_specs=[pl.BlockSpec(memory_space=pltpu.VMEM)] * 2,
        scratch_shapes=[
            v(4, 8, tok, dtype=F32), v(4, 8, tok, dtype=F32), v(4, chunk, 1, dtype=F32),
            v(HALVES, 4, chunk, part), v(HALVES, 4, chunk, part), v(HALVES, 4 * chunk, part),
            v(4, 4, chunk, sub), v(4, sub, 4 * chunk),
            v(4, 4, sub, sub), v(4, sub, 4 * sub),
            *trio, *line_trio, *trio, *trio,
            v(HALVES, 4, chunk, part), v(HALVES, 5, chunk, part),
            v(HALVES, sub, part, dtype=F32), v(HALVES, chunk, part, dtype=F32),
            v(4, HALVES, sub, part, dtype=F32), v(HALVES, chunk, part, dtype=F32),
            v(4, 4 * chunk, sub, dtype=F32),
            v(4, half, sub), v(4, half, sub),
            v(4, 4, quarter, sub), v(4, 4, quarter, sub),
            v(4, eighth, sub), v(4, eighth, sub),
            v(4, quarter, sub, dtype=F32), v(4, eighth, sub, dtype=F32), v(4, eighth, sub),
            pltpu.SemaphoreType.DMA((N_SEMS,)),
            pltpu.SemaphoreType.DMA((N_SEMS,)),
            pltpu.SemaphoreType.DMA((2,)),
        ],
        compiler_params=pltpu.CompilerParams(
            collective_id=0, has_side_effects=True, vmem_limit_bytes=60 * 1024 * 1024
        ),
        name="width_growth",
    )(
        tokens.T,
        norm_gain.reshape(16, chunk),
        expansion.reshape(4, 4, chunk, sub),
        small_weight.reshape(4, 4, sub, sub),
        cotangent.T,
    )
    return mixed.T, pieces.reshape(16 * chunk, sub).astype(F32)


def solution(mesh):
    in_specs = (P("dp", "fsdp"), P(), P(None, "fsdp"), P(None, "fsdp"), P("dp", "fsdp"))
    out_specs = (P("dp", "fsdp"), P(None, "fsdp"))
    return jax.shard_map(
        per_device, mesh=mesh, in_specs=in_specs, out_specs=out_specs, check_vma=False
    )
```

```python
import jax
import jax.numpy as jnp
from jax import lax
from jax.experimental import pallas as pl
from jax.experimental.pallas import tpu as pltpu
from jax.sharding import PartitionSpec as P

MESH = pl.DeviceIdType.MESH
F32 = jnp.float32
BF16 = jnp.bfloat16
N_SEMS = 256
HALVES = 2


def nn(a, b):
    return lax.dot_general(a, b, (((1,), (0,)), ((), ())), preferred_element_type=F32)


def nt(a, b):
    return lax.dot_general(a, b, (((1,), (1,)), ((), ())), preferred_element_type=F32)


def kernel(
    x_ref, gain_ref, e_ref, w_ref, c_ref, mixed_ref, fg,
    stat_x, stat_z, gain, gx, gc, normed, eb, ebt, wb, wbt,
    r_s, r_r, r_g, p_s, p_r, p_g, b_s, b_r, b_g, q_s, q_r, q_g,
    o_s, o_r, p_h, o_h, own, o_own, grad, gs, gr, ys, yr, zs, zr, y_own, z_own, x_s,
    ss, rs, ls,
):
    chunk, tok = x_ref.shape
    part = tok // HALVES
    sub = w_ref.shape[2]
    features = chunk * 16
    d, f = lax.axis_index("dp"), lax.axis_index("fsdp")
    y, h, c = d // 4, (d // 2) % 2, d % 2
    z, x = f // 4, f % 4

    def dev(y=y, h=h, c=c, z=z, x=x):
        return {"dp": y * 4 + h * 2 + c, "fsdp": z * 4 + x}

    def turn(v, k):
        return lax.rem(v + k + 4, 4)

    xp = [dev(x=turn(x, k)) for k in range(4)]
    zp = [dev(z=turn(z, k)) for k in range(4)]
    yp = [dev(y=turn(y, k)) for k in range(4)]
    hp, cp = dev(h=1 - h), dev(c=1 - c)

    barrier = pltpu.get_barrier_semaphore()
    xhp = [dev(x=turn(x, k), h=1 - h) for k in range(4)]
    friends = xp[1:] + zp[1:] + yp[1:] + xhp + [cp]
    for friend in friends:
        pl.semaphore_signal(barrier, inc=1, device_id=friend, device_id_type=MESH)
    pl.semaphore_wait(barrier, len(friends))

    counter = [0]
    pending = []
    lines = []

    def take(n):
        at = counter[0]
        counter[0] += n
        assert counter[0] <= N_SEMS
        return at

    def remote(src, dst, send_sem, recv_sem, to):
        return pltpu.make_async_remote_copy(
            src_ref=src, dst_ref=dst, send_sem=ss.at[send_sem], recv_sem=rs.at[recv_sem],
            device_id=to, device_id_type=MESH,
        )

    def send(src, dst, to):
        sem = take(1)
        copy = remote(src, dst, sem, sem, to)
        copy.start()
        pending.append(copy)
        return copy

    def arrive(copies):
        for copy in copies:
            copy.wait_recv()

    class Line:
        def __init__(self, own, slots):
            self.own, self.slots, self.sem = own, slots, take(5)
            lines.append(self)

        def sends(self):
            for way, (ok, to) in enumerate((
                (z < 3, z + 1), (z > 0, z - 1), (z < 2, z + 2), (z > 1, z - 2),
            )):
                to = jnp.clip(to, 0, 3)
                yield ok, remote(
                    self.own, self.slots.at[z], self.sem + way, self.sem + z, dev(z=to)
                )

        def handed(self):
            at = jnp.clip(3 * (2 - z), 0, 3)
            to = jnp.clip(3 * (z - 1), 0, 3)
            return at, remote(
                self.slots.at[at], self.slots.at[at], self.sem + 4, self.sem + at, dev(z=to)
            )

        def begin(self):
            for ok, copy in self.sends():
                @pl.when(ok)
                def _():
                    copy.start()

        def hand_over(self):
            @pl.when((z == 1) | (z == 2))
            def _():
                at, copy = self.handed()
                copy.wait_recv()
                copy.start()

        def arrive(self):
            for s in range(4):
                ok = z != s
                if s == 0:
                    ok = ok & (z != 2)
                if s == 3:
                    ok = ok & (z != 1)

                @pl.when(ok)
                def _():
                    block = self.slots.at[s]
                    remote(block, block, self.sem, self.sem + s, dev(z=turn(z, 1))).wait_recv()

        def finish(self):
            for ok, copy in self.sends():
                @pl.when(ok)
                def _():
                    copy.wait_send()

            @pl.when((z == 1) | (z == 2))
            def _():
                self.handed()[1].wait_send()

    class LineSum:
        def __init__(self, make, out, landed, held, mine):
            self.out, self.landed, self.held, self.mine = out, landed, held, mine
            self.sem = take(5)
            lines.append(self)
            for k in (3, 1):
                out[k] = make(turn(z, k)).astype(BF16)
                self.copy(k).start()
            held[...] = make(turn(z, 2))

            @pl.when((z == 0) | (z == 3))
            def _():
                out[2] = held[...].astype(BF16)
                self.copy(2).start()

            mine[...] = make(z)

        def copy(self, k):
            if k == 3:
                to, slot = jnp.where(z > 0, z - 1, 1), jnp.where(z > 0, z, 4)
            elif k == 1:
                to, slot = jnp.where(z < 3, z + 1, 2), jnp.where(z < 3, z, 4)
            else:
                to, slot = turn(z, 2), z
            return remote(
                self.out.at[k], self.landed.at[slot], self.sem + k, self.sem + slot, dev(z=to)
            )

        def landing(self, s):
            block = self.landed.at[s]
            return remote(block, block, self.sem, self.sem + s, dev(z=turn(z, 1)))

        def hand_over(self):
            @pl.when((z == 1) | (z == 2))
            def _():
                self.landing(4).wait_recv()
                total = self.held[...] + self.landed[4].astype(F32)
                self.out[2] = total.astype(BF16)
                self.copy(2).start()

        def collect(self):
            for s in range(4):
                ok = z != s
                if s in (0, 3):
                    ok = ok & (z != 3 - s)

                @pl.when(ok)
                def _():
                    self.landing(s).wait_recv()
                    self.mine[...] = self.mine[...] + self.landed[s].astype(F32)

            return self.mine[...]

        def finish(self):
            for k in (1, 2, 3):
                self.copy(k).wait_send()

    both = range(HALVES)

    def cut(ref, i):
        return ref.at[:, pl.ds(i * part, part)]

    line_x = [Line(cut(x_ref, i), gx.at[i]) for i in both]
    line_c = [Line(cut(c_ref, i), gc.at[i]) for i in both]
    line_x[0].begin()

    half = pl.ds(2 * c, 2)
    e_in = [send(e_ref.at[half, turn(x, k)], eb.at[x, half], xp[k]) for k in (1, 3, 2)]
    local_e = pltpu.make_async_copy(e_ref.at[:, x], eb.at[x], ls.at[0])
    local_w = pltpu.make_async_copy(w_ref.at[:, x], wb.at[x], ls.at[1])
    local_e.start()
    local_w.start()

    wide = x_ref[...].astype(F32)
    stat_x[0] = jnp.broadcast_to(jnp.sum(wide * wide, axis=0, keepdims=True), (8, tok))
    stat_a = [send(stat_x.at[0], stat_x.at[k], xp[k]) for k in (1, 2, 3)]
    for i in both[1:]:
        line_x[i].begin()
    for i in both:
        gx[i, z] = x_ref[:, i * part : (i + 1) * part]
        gc[i, z] = c_ref[:, i * part : (i + 1) * part]
    rows = lax.broadcasted_iota(jnp.int32, (chunk, chunk), 0)
    cols = lax.broadcasted_iota(jnp.int32, (chunk, chunk), 1)
    for j in range(4):
        at = (j * 2 + x // 2) * 5 + (x % 2) * 2
        line = jnp.concatenate([gain_ref[pl.ds(at + n, 1)] for n in range(3)], axis=1)
        line = jnp.where(x % 2 == 0, line[:, :chunk], line[:, 64 : 64 + chunk])
        gain[j] = jnp.sum(jnp.where(rows == cols, line, 0.0), axis=1, keepdims=True)
    arrive(stat_a)
    stat_z[0] = stat_x[0] + stat_x[1] + stat_x[2] + stat_x[3]
    stat_b = [send(stat_z.at[0], stat_z.at[k], zp[k]) for k in (1, 2, 3)]

    def turn_e(block):
        ebt[block] = jnp.transpose(eb[block].reshape(4 * chunk, sub))

    def turn_w(block):
        wbt[block] = jnp.transpose(wb[block].reshape(4 * sub, sub))

    local_e.wait()
    turn_e(x)
    line_x[0].hand_over()
    e_fwd = []
    for copy, k in zip(e_in, (1, 3, 2)):
        copy.wait_recv()
        at = turn(x, -k)
        e_fwd.append(send(eb.at[at, half], eb.at[at, half], cp))
    w_in = [send(w_ref.at[half, turn(x, k)], wb.at[x, half], xp[k]) for k in (1, 3, 2)]
    line_x[0].arrive()
    line_c[0].begin()
    arrive(stat_b)
    total = stat_z[0] + stat_z[1] + stat_z[2] + stat_z[3]
    scale = lax.rsqrt(total[0:1] * (1.0 / features) + 1e-05)

    def norm(i):
        for j in range(4):
            wide = gx[i, j].astype(F32) * scale[:, i * part : (i + 1) * part] * gain[j]
            normed[i, j * chunk : (j + 1) * chunk] = wide.astype(BF16)

    norm(0)
    line_x[1].hand_over()
    for copy, k in zip(e_fwd, (1, 3, 2)):
        copy.wait_recv()
        turn_e(turn(x, -k))

    def scatter(make, out, landed, mine, to):
        copies = []
        for k in (2, 1, 3):
            out[k] = make(k).astype(BF16)
            copies.append(send(out.at[k], landed.at[k], to[k]))
        mine[...] = make(0)
        return copies

    def collect(copies, landed, mine):
        total = mine[...]
        for copy, k in zip(copies, (2, 1, 3)):
            copy.wait_recv()
            total = total + landed[k].astype(F32)
        return total

    def share(slots, value):
        slots[x] = value.astype(BF16)
        return [send(slots.at[x], slots.at[x], xp[k]) for k in (2, 1, 3)]

    def stacked(block):
        return block.reshape(block.shape[0] * block.shape[1], block.shape[2])

    def scatter_r(i):
        return scatter(
            lambda k: nn(ebt[turn(x, k)], normed[i]), r_s.at[i], r_r.at[i], own.at[0, i], xp
        )

    def scatter_p(i):
        def make(at):
            total = nn(wb[0, at], r_g[i, 0])
            for j in range(1, 4):
                total = total + nn(wb[j, at], r_g[i, j])
            return total

        return LineSum(make, p_s.at[i], p_r.at[i], p_h.at[i], own.at[1, i])

    def scatter_b(i):
        return scatter(
            lambda k: nn(ebt[turn(x, k)], stacked(gc[i])),
            b_s.at[i], b_r.at[i], own.at[2, i], xp,
        )

    def scatter_q(i):
        return scatter(
            lambda k: nn(wbt[turn(x, k)], stacked(b_g[i])),
            q_s.at[i], q_r.at[i], own.at[3, i], xp,
        )

    def scatter_o(i):
        def make(at):
            total = nn(eb[0, at], p_g[i, 0])
            for j in range(1, 4):
                total = total + nn(eb[j, at], p_g[i, j])
            return total

        return LineSum(make, o_s.at[i], o_r.at[i], o_h.at[i], o_own.at[i])

    r_sum, r_all, p_sum, p_all = {}, {}, {}, {}
    b_sum, q_sum, q_all, o_sum = {}, {}, {}, {}
    r_sum[0] = scatter_r(0)
    line_x[1].arrive()
    line_c[1].begin()
    norm(1)
    r_sum[1] = scatter_r(1)
    line_c[0].hand_over()
    r_all[0] = share(r_g.at[0], collect(r_sum[0], r_r.at[0], own.at[0, 0]))
    local_w.wait()
    w_fwd = []
    for copy, k in zip(w_in, (1, 3, 2)):
        copy.wait_recv()
        at = turn(x, -k)
        w_fwd.append(send(wb.at[at, half], wb.at[at, half], cp))
    r_all[1] = share(r_g.at[1], collect(r_sum[1], r_r.at[1], own.at[0, 1]))
    line_c[0].arrive()
    arrive(w_fwd)

    arrive(r_all[0])
    p_sum[0] = scatter_p(0)
    line_c[1].hand_over()
    b_sum[0] = scatter_b(0)
    p_sum[0].hand_over()
    arrive(r_all[1])
    p_sum[1] = scatter_p(1)
    line_c[1].arrive()
    b_sum[1] = scatter_b(1)

    line_b = [Line(b_g.at[i, z], b_g.at[i]) for i in both]

    def gather_b(i):
        b_g[i, z] = collect(b_sum[i], b_r.at[i], own.at[2, i]).astype(BF16)
        line_b[i].begin()

    gather_b(0)
    p_sum[1].hand_over()
    p_all[0] = share(p_g.at[0], p_sum[0].collect())
    line_b[0].hand_over()
    gather_b(1)
    p_all[1] = share(p_g.at[1], p_sum[1].collect())
    for j in range(4):
        turn_w(j)

    line_b[0].arrive()
    q_sum[0] = scatter_q(0)
    line_b[1].hand_over()
    arrive(p_all[0])
    order = (0, 2, 1, 3)

    def cotangent_part(i, t):
        at = turn(x, -order[t])
        for j in range(4):
            rows = slice(j * chunk, (j + 1) * chunk)
            product = nt(gc[i, j], p_g[i, at])
            grad[t, rows] = product if i == 0 else grad[t, rows] + product

    o_sum[0] = scatter_o(0)
    line_b[1].arrive()
    q_sum[1] = scatter_q(1)
    arrive(p_all[1])
    o_sum[1] = scatter_o(1)
    q_all[0] = share(q_g.at[0], collect(q_sum[0], q_r.at[0], own.at[3, 0]))
    for i in both:
        cotangent_part(i, 0)
    q_all[1] = share(q_g.at[1], collect(q_sum[1], q_r.at[1], own.at[3, 1]))

    halves = 2 * chunk
    quarter, eighth = halves // 4, halves // 8
    stage = {}

    def grad_block(t):
        at = turn(x, -order[t])
        if t:
            for i in both:
                q_all[i][t - 1].wait_recv()
        away = pl.ds(pl.multiple_of((1 - c) * halves, halves), halves)
        home = pl.ds(pl.multiple_of(c * halves, halves), halves)

        def total(rows):
            value = grad[t, rows]
            for i in both:
                value = value + nt(normed[i, rows], q_g[i, at])
            return value

        gs[t] = total(away).astype(BF16)
        stage["c", t] = send(gs.at[t], gr.at[t], cp)
        grad[t, home] = total(home)

    def over_y(t):
        stage["c", t].wait_recv()
        copies = []
        for k in (2, 1, 3, 0):
            at = turn(y, k) * quarter
            mine = pl.ds(pl.multiple_of(c * halves + at, quarter), quarter)
            theirs = pl.ds(pl.multiple_of(at, quarter), quarter)
            total = grad[t, mine] + gr[t, theirs].astype(F32)
            if k:
                ys[t, k] = total.astype(BF16)
                copies.append(send(ys.at[t, k], yr.at[t, k], yp[k]))
            else:
                y_own[t] = total
        stage["y", t] = copies

    def over_h(t):
        arrive(stage["y", t])

        def share_of(at):
            rows = pl.ds(pl.multiple_of(at * eighth, eighth), eighth)
            total = y_own[t, rows]
            for k in (1, 2, 3):
                total = total + yr[t, k, rows].astype(F32)
            return total

        zs[t] = share_of(1 - h).astype(BF16)
        stage["h", t] = send(zs.at[t], zr.at[t], hp)
        z_own[t] = share_of(h)

    def piece(c, y, h):
        return c * 2 + y // 2, (y % 2) * 2 + h

    first, last = piece(c, y, h)

    def over_x(t):
        stage["h", t].wait_recv()
        total = (z_own[t] + zr[t].astype(F32)).astype(BF16)
        k = order[t]
        if k:
            x_s[t] = total
            stage["x", t] = send(x_s.at[t], fg.at[first, x, last], xp[(4 - k) % 4])
            stage["xh", t] = send(x_s.at[t], fg.at[first, x, last], xhp[(4 - k) % 4])
        else:
            fg[first, x, last] = total
            slot = fg.at[first, x, last]
            stage["xh", t] = send(slot, slot, hp)

    given = {}

    def give(t, at, to):
        block = turn(x, order[t])
        return send(fg.at[at[0], block, at[1]], fg.at[at[0], block, at[1]], to)

    from_c = []

    def out_own(t):
        if t:
            stage["x", t].wait_recv()
        at = piece(c, y, h)
        given["y", t, 0] = [give(t, at, yp[k]) for k in (2, 1, 3)]
        from_c.append(give(t, at, cp))

    def out_other(t):
        stage["xh", t].wait_recv()
        at = piece(c, y, 1 - h)
        given["y", t, 1] = [give(t, at, yp[k]) for k in (2, 1, 3)]
        from_c.append(give(t, at, cp))

    def out_core(t, other):
        for copy, k in zip(given["y", t, other], (2, 1, 3)):
            copy.wait_recv()
            from_c.append(give(t, piece(c, turn(y, -k), 1 - h if other else h), cp))

    def finish_mixed():
        for i in both:
            total = x_ref[:, i * part : (i + 1) * part].astype(F32)
            mixed_ref[:, i * part : (i + 1) * part] = (
                total + o_sum[i].collect()
            ).astype(BF16)

    grad_block(0)
    o_sum[0].hand_over()
    over_y(0)
    for t in (1, 2, 3):
        for i in both:
            cotangent_part(i, t)
    grad_block(1)
    o_sum[1].hand_over()
    grad_block(2)
    over_y(1)
    grad_block(3)
    over_h(0)
    over_y(2)
    over_x(0)
    out_own(0)
    over_h(1)
    over_y(3)
    over_h(2)
    over_x(1)
    out_other(0)
    over_h(3)
    over_x(2)
    out_own(1)
    out_core(0, 0)
    over_x(3)
    out_own(2)
    out_other(1)
    out_core(0, 1)
    out_own(3)
    out_core(1, 0)
    out_other(2)
    out_core(1, 1)
    out_core(2, 0)
    out_other(3)
    finish_mixed()
    out_core(2, 1)
    out_core(3, 0)
    out_core(3, 1)
    arrive(from_c)

    for line in lines:
        line.finish()
    for copy in pending:
        copy.wait_send()


def per_device(tokens, norm_gain, expansion, small_weight, cotangent):
    tok, chunk = tokens.shape
    sub = expansion.shape[1]
    half, eighth = 2 * chunk, chunk // 4
    quarter, part = half // 4, tok // HALVES

    def v(*shape, dtype=BF16):
        return pltpu.VMEM(shape, dtype)

    trio = [v(HALVES, 4, sub, part)] * 3
    line_trio = [v(HALVES, 4, sub, part), v(HALVES, 5, sub, part), v(HALVES, 4, sub, part)]
    mixed, pieces = pl.pallas_call(
        kernel,
        out_shape=[
            jax.ShapeDtypeStruct((chunk, tok), BF16),
            jax.ShapeDtypeStruct((4, 4, 4, eighth, sub), BF16),
        ],
        in_specs=[
            pl.BlockSpec(memory_space=pltpu.VMEM),
            pl.BlockSpec(memory_space=pltpu.VMEM),
            pl.BlockSpec(memory_space=pl.ANY),
            pl.BlockSpec(memory_space=pl.ANY),
            pl.BlockSpec(memory_space=pltpu.VMEM),
        ],
        out_specs=[pl.BlockSpec(memory_space=pltpu.VMEM)] * 2,
        scratch_shapes=[
            v(4, 8, tok, dtype=F32), v(4, 8, tok, dtype=F32), v(4, chunk, 1, dtype=F32),
            v(HALVES, 4, chunk, part), v(HALVES, 4, chunk, part), v(HALVES, 4 * chunk, part),
            v(4, 4, chunk, sub), v(4, sub, 4 * chunk),
            v(4, 4, sub, sub), v(4, sub, 4 * sub),
            *trio, *line_trio, *trio, *trio,
            v(HALVES, 4, chunk, part), v(HALVES, 5, chunk, part),
            v(HALVES, sub, part, dtype=F32), v(HALVES, chunk, part, dtype=F32),
            v(4, HALVES, sub, part, dtype=F32), v(HALVES, chunk, part, dtype=F32),
            v(4, 4 * chunk, sub, dtype=F32),
            v(4, half, sub), v(4, half, sub),
            v(4, 4, quarter, sub), v(4, 4, quarter, sub),
            v(4, eighth, sub), v(4, eighth, sub),
            v(4, quarter, sub, dtype=F32), v(4, eighth, sub, dtype=F32), v(4, eighth, sub),
            pltpu.SemaphoreType.DMA((N_SEMS,)),
            pltpu.SemaphoreType.DMA((N_SEMS,)),
            pltpu.SemaphoreType.DMA((2,)),
        ],
        compiler_params=pltpu.CompilerParams(
            collective_id=0, has_side_effects=True, vmem_limit_bytes=60 * 1024 * 1024
        ),
        name="width_growth",
    )(
        tokens.T,
        norm_gain.reshape(chunk // 8, 128),
        expansion.reshape(4, 4, chunk, sub),
        small_weight.reshape(4, 4, sub, sub),
        cotangent.T,
    )
    return mixed.T, pieces.reshape(16 * chunk, sub).astype(F32)


def solution(mesh):
    in_specs = (P("dp", "fsdp"), P(), P(None, "fsdp"), P(None, "fsdp"), P("dp", "fsdp"))
    out_specs = (P("dp", "fsdp"), P(None, "fsdp"))
    return jax.shard_map(
        per_device, mesh=mesh, in_specs=in_specs, out_specs=out_specs, check_vma=False
    )
```

```python
import jax
import jax.numpy as jnp
from jax import lax
from jax.experimental import pallas as pl
from jax.experimental.pallas import tpu as pltpu
from jax.sharding import PartitionSpec as P

MESH = pl.DeviceIdType.MESH
F32 = jnp.float32
BF16 = jnp.bfloat16
N_SEMS = 256
HALVES = 2


def nn(a, b):
    return lax.dot_general(a, b, (((1,), (0,)), ((), ())), preferred_element_type=F32)


def nt(a, b):
    return lax.dot_general(a, b, (((1,), (1,)), ((), ())), preferred_element_type=F32)


def kernel(
    x_ref, gain_ref, e_ref, w_ref, c_ref, mixed_ref, fg,
    stat_x, stat_z, gain, gx, gc, normed, eb, ebt, wb, wbt,
    r_s, r_r, r_g, p_s, p_r, p_g, b_s, b_r, b_g, q_s, q_r, q_g,
    o_s, o_r, p_h, o_h, own, o_own, grad, gs, gr, ys, yr, zs, zr, y_own, z_own, x_s,
    ss, rs, ls,
):
    chunk, tok = x_ref.shape
    part = tok // HALVES
    sub = w_ref.shape[2]
    features = chunk * 16
    d, f = lax.axis_index("dp"), lax.axis_index("fsdp")
    y, h, c = d // 4, (d // 2) % 2, d % 2
    z, x = f // 4, f % 4

    def dev(y=y, h=h, c=c, z=z, x=x):
        return {"dp": y * 4 + h * 2 + c, "fsdp": z * 4 + x}

    def turn(v, k):
        return lax.rem(v + k + 4, 4)

    xp = [dev(x=turn(x, k)) for k in range(4)]
    zp = [dev(z=turn(z, k)) for k in range(4)]
    yp = [dev(y=turn(y, k)) for k in range(4)]
    hp, cp = dev(h=1 - h), dev(c=1 - c)

    barrier = pltpu.get_barrier_semaphore()
    xhp = [dev(x=turn(x, k), h=1 - h) for k in range(4)]
    friends = xp[1:] + zp[1:] + yp[1:] + xhp + [cp]
    for friend in friends:
        pl.semaphore_signal(barrier, inc=1, device_id=friend, device_id_type=MESH)
    pl.semaphore_wait(barrier, len(friends))

    counter = [0]
    pending = []
    lines = []

    def take(n):
        at = counter[0]
        counter[0] += n
        assert counter[0] <= N_SEMS
        return at

    def remote(src, dst, send_sem, recv_sem, to):
        return pltpu.make_async_remote_copy(
            src_ref=src, dst_ref=dst, send_sem=ss.at[send_sem], recv_sem=rs.at[recv_sem],
            device_id=to, device_id_type=MESH,
        )

    def send(src, dst, to):
        sem = take(1)
        copy = remote(src, dst, sem, sem, to)
        copy.start()
        pending.append(copy)
        return copy

    def arrive(copies):
        for copy in copies:
            copy.wait_recv()

    class Line:
        def __init__(self, own, slots):
            self.own, self.slots, self.sem = own, slots, take(5)
            lines.append(self)

        def sends(self):
            for way, (ok, to) in enumerate((
                (z < 3, z + 1), (z > 0, z - 1), (z < 2, z + 2), (z > 1, z - 2),
            )):
                to = jnp.clip(to, 0, 3)
                yield ok, remote(
                    self.own, self.slots.at[z], self.sem + way, self.sem + z, dev(z=to)
                )

        def handed(self):
            at = jnp.clip(3 * (2 - z), 0, 3)
            to = jnp.clip(3 * (z - 1), 0, 3)
            return at, remote(
                self.slots.at[at], self.slots.at[at], self.sem + 4, self.sem + at, dev(z=to)
            )

        def begin(self):
            for ok, copy in self.sends():
                @pl.when(ok)
                def _():
                    copy.start()

        def hand_over(self):
            @pl.when((z == 1) | (z == 2))
            def _():
                at, copy = self.handed()
                copy.wait_recv()
                copy.start()

        def arrive(self):
            for s in range(4):
                ok = z != s
                if s == 0:
                    ok = ok & (z != 2)
                if s == 3:
                    ok = ok & (z != 1)

                @pl.when(ok)
                def _():
                    block = self.slots.at[s]
                    remote(block, block, self.sem, self.sem + s, dev(z=turn(z, 1))).wait_recv()

        def finish(self):
            for ok, copy in self.sends():
                @pl.when(ok)
                def _():
                    copy.wait_send()

            @pl.when((z == 1) | (z == 2))
            def _():
                self.handed()[1].wait_send()

    class LineSum:
        def __init__(self, make, out, landed, held, mine):
            self.out, self.landed, self.held, self.mine = out, landed, held, mine
            self.sem = take(5)
            lines.append(self)
            for k in (3, 1):
                out[k] = make(turn(z, k)).astype(BF16)
                self.copy(k).start()
            held[...] = make(turn(z, 2))

            @pl.when((z == 0) | (z == 3))
            def _():
                out[2] = held[...].astype(BF16)
                self.copy(2).start()

            mine[...] = make(z)

        def copy(self, k):
            if k == 3:
                to, slot = jnp.where(z > 0, z - 1, 1), jnp.where(z > 0, z, 4)
            elif k == 1:
                to, slot = jnp.where(z < 3, z + 1, 2), jnp.where(z < 3, z, 4)
            else:
                to, slot = turn(z, 2), z
            return remote(
                self.out.at[k], self.landed.at[slot], self.sem + k, self.sem + slot, dev(z=to)
            )

        def landing(self, s):
            block = self.landed.at[s]
            return remote(block, block, self.sem, self.sem + s, dev(z=turn(z, 1)))

        def hand_over(self):
            @pl.when((z == 1) | (z == 2))
            def _():
                self.landing(4).wait_recv()
                total = self.held[...] + self.landed[4].astype(F32)
                self.out[2] = total.astype(BF16)
                self.copy(2).start()

        def collect(self):
            for s in range(4):
                ok = z != s
                if s in (0, 3):
                    ok = ok & (z != 3 - s)

                @pl.when(ok)
                def _():
                    self.landing(s).wait_recv()
                    self.mine[...] = self.mine[...] + self.landed[s].astype(F32)

            return self.mine[...]

        def finish(self):
            for k in (1, 2, 3):
                self.copy(k).wait_send()

    both = range(HALVES)

    def cut(ref, i):
        return ref.at[:, pl.ds(i * part, part)]

    line_x = [Line(cut(x_ref, i), gx.at[i]) for i in both]
    line_c = [Line(cut(c_ref, i), gc.at[i]) for i in both]
    line_x[0].begin()

    half = pl.ds(2 * c, 2)
    e_in = [send(e_ref.at[half, turn(x, k)], eb.at[x, half], xp[k]) for k in (1, 3, 2)]
    local_e = pltpu.make_async_copy(e_ref.at[:, x], eb.at[x], ls.at[0])
    local_w = pltpu.make_async_copy(w_ref.at[:, x], wb.at[x], ls.at[1])
    local_e.start()
    local_w.start()

    wide = x_ref[...].astype(F32)
    stat_x[0] = jnp.broadcast_to(jnp.sum(wide * wide, axis=0, keepdims=True), (8, tok))
    stat_a = [send(stat_x.at[0], stat_x.at[k], xp[k]) for k in (1, 2, 3)]
    for i in both[1:]:
        line_x[i].begin()
    for i in both:
        gx[i, z] = x_ref[:, i * part : (i + 1) * part]
        gc[i, z] = c_ref[:, i * part : (i + 1) * part]
    rows = lax.broadcasted_iota(jnp.int32, (chunk, chunk), 0)
    cols = lax.broadcasted_iota(jnp.int32, (chunk, chunk), 1)
    for j in range(4):
        at = (j * 2 + x // 2) * 5 + (x % 2) * 2
        line = jnp.concatenate([gain_ref[pl.ds(at + n, 1)] for n in range(3)], axis=1)
        line = jnp.where(x % 2 == 0, line[:, :chunk], line[:, 64 : 64 + chunk])
        gain[j] = jnp.sum(jnp.where(rows == cols, line, 0.0), axis=1, keepdims=True)
    arrive(stat_a)
    stat_z[0] = stat_x[0] + stat_x[1] + stat_x[2] + stat_x[3]
    stat_b = [send(stat_z.at[0], stat_z.at[k], zp[k]) for k in (1, 2, 3)]

    def turn_e(block):
        ebt[block] = jnp.transpose(eb[block].reshape(4 * chunk, sub))

    def turn_w(block):
        wbt[block] = jnp.transpose(wb[block].reshape(4 * sub, sub))

    local_e.wait()
    turn_e(x)
    line_x[0].hand_over()
    line_c[0].begin()
    e_fwd = []
    for copy, k in zip(e_in, (1, 3, 2)):
        copy.wait_recv()
        at = turn(x, -k)
        e_fwd.append(send(eb.at[at, half], eb.at[at, half], cp))
    w_in = [send(w_ref.at[half, turn(x, k)], wb.at[x, half], xp[k]) for k in (1, 3, 2)]
    line_x[0].arrive()
    arrive(stat_b)
    total = stat_z[0] + stat_z[1] + stat_z[2] + stat_z[3]
    scale = lax.rsqrt(total[0:1] * (1.0 / features) + 1e-05)

    def norm(i):
        for j in range(4):
            wide = gx[i, j].astype(F32) * scale[:, i * part : (i + 1) * part] * gain[j]
            normed[i, j * chunk : (j + 1) * chunk] = wide.astype(BF16)

    norm(0)
    line_x[1].hand_over()
    for copy, k in zip(e_fwd, (1, 3, 2)):
        copy.wait_recv()
        turn_e(turn(x, -k))

    def scatter(make, out, landed, mine, to):
        copies = []
        for k in (2, 1, 3):
            out[k] = make(k).astype(BF16)
            copies.append(send(out.at[k], landed.at[k], to[k]))
        mine[...] = make(0)
        return copies

    def collect(copies, landed, mine):
        total = mine[...]
        for copy, k in zip(copies, (2, 1, 3)):
            copy.wait_recv()
            total = total + landed[k].astype(F32)
        return total

    def share(slots, value):
        slots[x] = value.astype(BF16)
        return [send(slots.at[x], slots.at[x], xp[k]) for k in (2, 1, 3)]

    def stacked(block):
        return block.reshape(block.shape[0] * block.shape[1], block.shape[2])

    def scatter_r(i):
        return scatter(
            lambda k: nn(ebt[turn(x, k)], normed[i]), r_s.at[i], r_r.at[i], own.at[0, i], xp
        )

    def scatter_p(i):
        def make(at):
            total = nn(wb[0, at], r_g[i, 0])
            for j in range(1, 4):
                total = total + nn(wb[j, at], r_g[i, j])
            return total

        return LineSum(make, p_s.at[i], p_r.at[i], p_h.at[i], own.at[1, i])

    def scatter_b(i):
        return scatter(
            lambda k: nn(ebt[turn(x, k)], stacked(gc[i])),
            b_s.at[i], b_r.at[i], own.at[2, i], xp,
        )

    def scatter_q(i):
        return scatter(
            lambda k: nn(wbt[turn(x, k)], stacked(b_g[i])),
            q_s.at[i], q_r.at[i], own.at[3, i], xp,
        )

    def scatter_o(i):
        def make(at):
            total = nn(eb[0, at], p_g[i, 0])
            for j in range(1, 4):
                total = total + nn(eb[j, at], p_g[i, j])
            return total

        return LineSum(make, o_s.at[i], o_r.at[i], o_h.at[i], o_own.at[i])

    r_sum, r_all, p_sum, p_all = {}, {}, {}, {}
    b_sum, q_sum, q_all, o_sum = {}, {}, {}, {}
    r_sum[0] = scatter_r(0)
    line_x[1].arrive()
    line_c[1].begin()
    norm(1)
    r_sum[1] = scatter_r(1)
    line_c[0].hand_over()
    r_all[0] = share(r_g.at[0], collect(r_sum[0], r_r.at[0], own.at[0, 0]))
    local_w.wait()
    w_fwd = []
    for copy, k in zip(w_in, (1, 3, 2)):
        copy.wait_recv()
        at = turn(x, -k)
        w_fwd.append(send(wb.at[at, half], wb.at[at, half], cp))
    r_all[1] = share(r_g.at[1], collect(r_sum[1], r_r.at[1], own.at[0, 1]))
    line_c[0].arrive()
    arrive(w_fwd)

    arrive(r_all[0])
    p_sum[0] = scatter_p(0)
    line_c[1].hand_over()
    b_sum[0] = scatter_b(0)
    p_sum[0].hand_over()
    arrive(r_all[1])
    p_sum[1] = scatter_p(1)
    line_c[1].arrive()
    b_sum[1] = scatter_b(1)

    line_b = [Line(b_g.at[i, z], b_g.at[i]) for i in both]

    def gather_b(i):
        b_g[i, z] = collect(b_sum[i], b_r.at[i], own.at[2, i]).astype(BF16)
        line_b[i].begin()

    gather_b(0)
    p_sum[1].hand_over()
    p_all[0] = share(p_g.at[0], p_sum[0].collect())
    line_b[0].hand_over()
    gather_b(1)
    p_all[1] = share(p_g.at[1], p_sum[1].collect())
    for j in range(4):
        turn_w(j)

    line_b[0].arrive()
    q_sum[0] = scatter_q(0)
    line_b[1].hand_over()
    arrive(p_all[0])
    order = (0, 2, 1, 3)

    def cotangent_part(i, t):
        at = turn(x, -order[t])
        for j in range(4):
            rows = slice(j * chunk, (j + 1) * chunk)
            product = nt(gc[i, j], p_g[i, at])
            grad[t, rows] = product if i == 0 else grad[t, rows] + product

    o_sum[0] = scatter_o(0)
    for t in range(4):
        cotangent_part(0, t)
    line_b[1].arrive()
    q_sum[1] = scatter_q(1)
    q_all[0] = share(q_g.at[0], collect(q_sum[0], q_r.at[0], own.at[3, 0]))
    arrive(p_all[1])
    cotangent_part(1, 0)
    o_sum[1] = scatter_o(1)
    q_all[1] = share(q_g.at[1], collect(q_sum[1], q_r.at[1], own.at[3, 1]))

    halves = 2 * chunk
    quarter, eighth = halves // 4, halves // 8
    stage = {}

    def grad_block(t):
        at = turn(x, -order[t])
        if t:
            for i in both:
                q_all[i][t - 1].wait_recv()
        away = pl.ds(pl.multiple_of((1 - c) * halves, halves), halves)
        home = pl.ds(pl.multiple_of(c * halves, halves), halves)

        def total(rows):
            value = grad[t, rows]
            for i in both:
                value = value + nt(normed[i, rows], q_g[i, at])
            return value

        gs[t] = total(away).astype(BF16)
        stage["c", t] = send(gs.at[t], gr.at[t], cp)
        grad[t, home] = total(home)

    def over_y(t):
        stage["c", t].wait_recv()
        copies = []
        for k in (2, 1, 3, 0):
            at = turn(y, k) * quarter
            mine = pl.ds(pl.multiple_of(c * halves + at, quarter), quarter)
            theirs = pl.ds(pl.multiple_of(at, quarter), quarter)
            total = grad[t, mine] + gr[t, theirs].astype(F32)
            if k:
                ys[t, k] = total.astype(BF16)
                copies.append(send(ys.at[t, k], yr.at[t, k], yp[k]))
            else:
                y_own[t] = total
        stage["y", t] = copies

    def over_h(t):
        arrive(stage["y", t])

        def share_of(at):
            rows = pl.ds(pl.multiple_of(at * eighth, eighth), eighth)
            total = y_own[t, rows]
            for k in (1, 2, 3):
                total = total + yr[t, k, rows].astype(F32)
            return total

        zs[t] = share_of(1 - h).astype(BF16)
        stage["h", t] = send(zs.at[t], zr.at[t], hp)
        z_own[t] = share_of(h)

    def piece(c, y, h):
        return c * 2 + y // 2, (y % 2) * 2 + h

    first, last = piece(c, y, h)

    def over_x(t):
        stage["h", t].wait_recv()
        total = (z_own[t] + zr[t].astype(F32)).astype(BF16)
        k = order[t]
        if k:
            x_s[t] = total
            stage["x", t] = send(x_s.at[t], fg.at[first, x, last], xp[(4 - k) % 4])
            stage["xh", t] = send(x_s.at[t], fg.at[first, x, last], xhp[(4 - k) % 4])
        else:
            fg[first, x, last] = total
            slot = fg.at[first, x, last]
            stage["xh", t] = send(slot, slot, hp)

    given = {}

    def give(t, at, to):
        block = turn(x, order[t])
        return send(fg.at[at[0], block, at[1]], fg.at[at[0], block, at[1]], to)

    from_c = []

    def out_own(t):
        if t:
            stage["x", t].wait_recv()
        at = piece(c, y, h)
        given["y", t, 0] = [give(t, at, yp[k]) for k in (2, 1, 3)]
        from_c.append(give(t, at, cp))

    def out_other(t):
        stage["xh", t].wait_recv()
        at = piece(c, y, 1 - h)
        given["y", t, 1] = [give(t, at, yp[k]) for k in (2, 1, 3)]
        from_c.append(give(t, at, cp))

    def out_core(t, other):
        for copy, k in zip(given["y", t, other], (2, 1, 3)):
            copy.wait_recv()
            from_c.append(give(t, piece(c, turn(y, -k), 1 - h if other else h), cp))

    def finish_mixed():
        for i in both:
            total = x_ref[:, i * part : (i + 1) * part].astype(F32)
            mixed_ref[:, i * part : (i + 1) * part] = (
                total + o_sum[i].collect()
            ).astype(BF16)

    grad_block(0)
    o_sum[0].hand_over()
    over_y(0)
    for t in (1, 2, 3):
        cotangent_part(1, t)
    grad_block(1)
    o_sum[1].hand_over()
    grad_block(2)
    over_y(1)
    grad_block(3)
    over_h(0)
    over_y(2)
    over_x(0)
    over_h(1)
    over_y(3)
    out_own(0)
    over_h(2)
    over_x(1)
    out_other(0)
    over_h(3)
    over_x(2)
    out_own(1)
    over_x(3)
    out_core(0, 0)
    out_own(2)
    out_other(1)
    out_core(0, 1)
    out_own(3)
    out_core(1, 0)
    out_other(2)
    out_core(1, 1)
    out_core(2, 0)
    out_other(3)
    finish_mixed()
    out_core(2, 1)
    out_core(3, 0)
    out_core(3, 1)
    arrive(from_c)

    for line in lines:
        line.finish()
    for copy in pending:
        copy.wait_send()


def per_device(tokens, norm_gain, expansion, small_weight, cotangent):
    tok, chunk = tokens.shape
    sub = expansion.shape[1]
    half, eighth = 2 * chunk, chunk // 4
    quarter, part = half // 4, tok // HALVES

    def v(*shape, dtype=BF16):
        return pltpu.VMEM(shape, dtype)

    trio = [v(HALVES, 4, sub, part)] * 3
    line_trio = [v(HALVES, 4, sub, part), v(HALVES, 5, sub, part), v(HALVES, 4, sub, part)]
    mixed, pieces = pl.pallas_call(
        kernel,
        out_shape=[
            jax.ShapeDtypeStruct((chunk, tok), BF16),
            jax.ShapeDtypeStruct((4, 4, 4, eighth, sub), BF16),
        ],
        in_specs=[
            pl.BlockSpec(memory_space=pltpu.VMEM),
            pl.BlockSpec(memory_space=pltpu.VMEM),
            pl.BlockSpec(memory_space=pl.ANY),
            pl.BlockSpec(memory_space=pl.ANY),
            pl.BlockSpec(memory_space=pltpu.VMEM),
        ],
        out_specs=[pl.BlockSpec(memory_space=pltpu.VMEM)] * 2,
        scratch_shapes=[
            v(4, 8, tok, dtype=F32), v(4, 8, tok, dtype=F32), v(4, chunk, 1, dtype=F32),
            v(HALVES, 4, chunk, part), v(HALVES, 4, chunk, part), v(HALVES, 4 * chunk, part),
            v(4, 4, chunk, sub), v(4, sub, 4 * chunk),
            v(4, 4, sub, sub), v(4, sub, 4 * sub),
            *trio, *line_trio, *trio, *trio,
            v(HALVES, 4, chunk, part), v(HALVES, 5, chunk, part),
            v(HALVES, sub, part, dtype=F32), v(HALVES, chunk, part, dtype=F32),
            v(4, HALVES, sub, part, dtype=F32), v(HALVES, chunk, part, dtype=F32),
            v(4, 4 * chunk, sub, dtype=F32),
            v(4, half, sub), v(4, half, sub),
            v(4, 4, quarter, sub), v(4, 4, quarter, sub),
            v(4, eighth, sub), v(4, eighth, sub),
            v(4, quarter, sub, dtype=F32), v(4, eighth, sub, dtype=F32), v(4, eighth, sub),
            pltpu.SemaphoreType.DMA((N_SEMS,)),
            pltpu.SemaphoreType.DMA((N_SEMS,)),
            pltpu.SemaphoreType.DMA((2,)),
        ],
        compiler_params=pltpu.CompilerParams(
            collective_id=0, has_side_effects=True, vmem_limit_bytes=60 * 1024 * 1024
        ),
        name="width_growth",
    )(
        tokens.T,
        norm_gain.reshape(chunk // 8, 128),
        expansion.reshape(4, 4, chunk, sub),
        small_weight.reshape(4, 4, sub, sub),
        cotangent.T,
    )
    return mixed.T, pieces.reshape(16 * chunk, sub).astype(F32)


def solution(mesh):
    in_specs = (P("dp", "fsdp"), P(), P(None, "fsdp"), P(None, "fsdp"), P("dp", "fsdp"))
    out_specs = (P("dp", "fsdp"), P(None, "fsdp"))
    return jax.shard_map(
        per_device, mesh=mesh, in_specs=in_specs, out_specs=out_specs, check_vma=False
    )
```
